32 devices in a mesh: frames: 2 (over y), bricks: 16 (over z, x, core).
Axes of the slice: x: 2, y: 2, z: 4, core: 2. Of those that a mesh axis runs over, the one named last changes fastest.
Arguments:
- recording: bfloat16 [32, 64, 16, 256], P('frames', 'bricks'), may hold values from -1 to 2
- traces: bfloat16 [32, 512], P('frames', 'bricks'), may hold values from 0 to 2
- footprints: bfloat16 [512, 16384], P('bricks'), may hold values from 0 to 1, as said below
- block_owner: int32 [512, 1], P('bricks'), may hold values from 0 to 15; in each aligned block of 32 rows (0 to 31, 32 to 63, ...) at most 4 rows name the same one
- block_slot: int32 [512], P('bricks'), may hold values from 0 to 31
Outputs:
- traces_new: float32 [32, 512], P('frames', 'bricks')
- footprints_new: bfloat16 [512, 16384], P('bricks')
The draws below stay inside these ranges and needn't reach their ends.
Inputs may be any that keep to these rules, and one draw needn't show every extreme that they name: `footprints`: each row is positive on exactly 128 voxels forming a run in the slab's flat voxel order taken circularly, and 0 elsewhere; positive entries are at least 0.02. `block_owner`: among the 32 blocks of one slab, at most 4 have the same owner.
All inputs are finite; a program needn't handle non-finite values.
Results may differ from the reference program's by a relative error of at most 0.0033.
Values may be sent and summed in bfloat16 or wider, within the bound.
A program may use at most 64 MiB of HBM per device.

```python
import math
import jax
import jax.numpy as jnp
import numpy as np
from jax import lax

NZ = 16
NY = 256
K_LOC = 32
FOOT_W = 128
COMP_DEV = 32
SEND_CAP = 4
NF = 32
NX = 64
V_DEV = 16384
NCOMP = 512
BLOCKS = 512
OWNERS = 16
N_BRICKS = 16


def draw_footprints(key, part):
    key_center, key_value = jax.random.split(jax.random.fold_in(key, 17))
    centers = jax.random.randint(key_center, (BLOCKS, 1), 0, V_DEV)
    offsets = (jnp.arange(V_DEV, dtype=jnp.int32)[None, :] - centers) % V_DEV
    inside = offsets < FOOT_W
    values = jnp.exp(jax.random.uniform(key_value, (BLOCKS, V_DEV), jnp.float32, math.log(0.02), 0.0))
    return jnp.where(inside, values, 0.0).astype(jnp.bfloat16)


def place_ends(drawn, stream_key, smallest, largest):
    longest = drawn.shape.index(max(drawn.shape))
    spots = []
    for shift in (0, 1):
        where = [jax.random.randint(jax.random.fold_in(stream_key, axis), (), 0, length) for axis, length in enumerate(drawn.shape)]
        where[longest] = (where[longest] + shift) % drawn.shape[longest]
        spots.append(tuple(where))
    return drawn.at[spots[0]].set(smallest).at[spots[1]].set(largest)


def steps_of(key, extent, pieces, low, largest):
    def one(position, blocks):
        steps = jax.random.uniform(jax.random.fold_in(jax.random.fold_in(key, 6), position), (blocks,), jnp.float32, low / len(pieces), largest / len(pieces))
        return jnp.repeat(jnp.exp(steps), extent[position] // blocks).reshape((-1,) + (1,) * (len(extent) - position - 1))

    level = one(*pieces[0])
    for cut in pieces[1:]:
        level = level * one(*cut)
    return level


def shared_out(rng, own, number, rows, amount, top, bound, lean):
    ranking = jax.random.permutation(rng, amount)
    heavy_load, ordinary = portions_of(amount, rows * top, bound, lean, True), portions_of(amount, rows * top, bound, lean, False)
    places = jnp.arange(amount)

    def named(sizes, offset_by):
        used = int((sizes > 0).sum())
        fixed = max(1, used // 4)
        passed = fixed + (places - fixed + offset_by * (used - fixed)) % max(1, amount - fixed)
        return jnp.zeros((amount,), jnp.int32).at[ranking[jnp.where(places < fixed, places, passed)]].set(jnp.asarray(sizes, jnp.int32))

    sizes = jnp.where(number % 4 == 0, named(heavy_load, number // 4), named(ordinary, number - number // 4 - 1))
    mixed = jax.random.permutation(jax.random.fold_in(own, 3), amount)
    source_of, sink = mixed[0:amount // 2 * 2:2], mixed[1:amount // 2 * 2:2]
    margin = jnp.minimum(sizes[source_of] - 1, bound - sizes[sink]) // 2
    margin = jnp.where((source_of == ranking[0]) | (sink == ranking[0]) | (sizes[sink] == 0), 0, jnp.maximum(margin, 0))
    passed = jax.random.randint(jax.random.fold_in(own, 4), (amount // 2,), 0, 1 << 20) % (margin + 1)
    sizes = sizes.at[source_of].add(-passed).at[sink].add(passed)
    labels = jnp.searchsorted(jnp.cumsum(sizes), jnp.arange(rows * top), side="right").astype(jnp.int32)
    table = labels.reshape(top, rows).T
    table = table[jax.random.permutation(jax.random.fold_in(own, 1), rows)]
    offset_by = jax.random.randint(jax.random.fold_in(own, 2), (rows, 1), 0, top)
    return jnp.take_along_axis(table, (jnp.arange(top)[None, :] + offset_by) % top, axis=1)


def portions_of(count, total, most, skew, full):
    weights = [(1 << 20) // math.isqrt(rank ** skew) + 1 for rank in range(1, count + 1)]
    largest = most if full else min(most, max(-(-total // count), total * weights[0] // sum(weights)))
    least = 1 if total - largest >= count - 1 else 0
    given, spare = [largest] + [least] * (count - 1), total - largest - least * (count - 1)
    while spare > 0:
        free = [i for i in range(1, count) if given[i] < largest] or [i for i in range(1, count) if given[i] < most]
        whole, left = sum([weights[i] for i in free]), spare
        for i in free:
            more = min(most - given[i], max(1, left * weights[i] // whole), spare)
            given[i] = given[i] + more
            spare = spare - more
    return np.array(given)


def setup_inputs(seed: int = 0) -> dict:
    key_of = jax.random.split(jax.random.key(seed), 6)
    recording = jnp.clip(-1.0 + 3.0 * jax.random.uniform(key_of[0], (NF, NX, NZ, NY), jnp.float32) ** steps_of(key_of[0], (NF, NX, NZ, NY), ((0, 2), (1, 16)), -0.2, 0.2), -1.0, 2.0).astype(jnp.bfloat16)
    traces = jnp.clip(2.0 * jax.random.uniform(key_of[1], (NF, NCOMP), jnp.float32) ** steps_of(key_of[1], (NF, NCOMP), ((0, 2), (1, 16)), -0.2, 0.2), 0.0, 2.0).astype(jnp.bfloat16)
    footprints = draw_footprints(jax.random.fold_in(key_of[5], 71), 0)
    block_owner_keys = jax.random.split(jax.random.fold_in(key_of[3], 1), BLOCKS // K_LOC)
    block_owner_turns = jax.random.permutation(jax.random.fold_in(key_of[3], 3), BLOCKS // K_LOC)
    block_owner = jax.vmap(lambda own, number: shared_out(jax.random.fold_in(key_of[3], 2), own, number, K_LOC, OWNERS, 1, SEND_CAP, 2))(block_owner_keys, block_owner_turns).reshape((BLOCKS, 1))
    block_slot = place_ends(jax.random.randint(key_of[4], (BLOCKS,), 0, COMP_DEV), jax.random.fold_in(key_of[4], 1), 0, COMP_DEV - 1).astype(jnp.int32)
    return dict(recording=recording, traces=traces, footprints=footprints, block_owner=block_owner, block_slot=block_slot)


TIME_STEP = 0.14
EDGE_SCALE = 1.0


def edge_flux(center, other):
    difference = other - center
    return difference / (1.0 + (difference / EDGE_SCALE) ** 2)


def relax_once(extended):
    center = extended[:, 1:-1]
    padded = jnp.pad(center, ((0, 0), (0, 0), (1, 1), (1, 1)))
    summed_flux = edge_flux(center, extended[:, 2:]) + edge_flux(center, extended[:, :-2])
    summed_flux = summed_flux + edge_flux(center, padded[:, :, 2:, 1:-1]) + edge_flux(center, padded[:, :, :-2, 1:-1])
    summed_flux = summed_flux + edge_flux(center, padded[:, :, 1:-1, 2:]) + edge_flux(center, padded[:, :, 1:-1, :-2])
    return center + TIME_STEP * summed_flux


def smooth_frame(frame):
    current = frame[None].astype(jnp.float32)
    for sweep in range(3):
        extended = jnp.pad(current, ((0, 0), (1, 1), (0, 0), (0, 0)))
        current = relax_once(extended)
    return current[0].astype(jnp.bfloat16)


def reference(recording, traces, footprints, block_owner, block_slot):
    denoised = lax.map(smooth_frame, recording)
    slabs = denoised.reshape(NF, N_BRICKS, V_DEV)
    component = (block_owner[:, 0] * COMP_DEV + block_slot).astype(jnp.int32)
    comp_grid = component.reshape(N_BRICKS, K_LOC)
    foot_grid = footprints.reshape(N_BRICKS, K_LOC, V_DEV)
    previous = traces.astype(jnp.float32)

    def brick_partials(brick_index):
        slab_data = lax.dynamic_index_in_dim(slabs, brick_index, 1, keepdims=False)
        foot = foot_grid[brick_index]
        slot_traces = jnp.take(previous, comp_grid[brick_index], axis=1)
        correlation = jnp.dot(foot, foot.T, preferred_element_type=jnp.float32)
        partial_value = jnp.dot(slab_data, foot.T, preferred_element_type=jnp.float32) - jnp.dot(slot_traces, correlation, precision=lax.Precision.HIGHEST)
        return partial_value.T, jnp.diagonal(correlation)

    partial_rows, diag_rows = lax.map(brick_partials, jnp.arange(N_BRICKS, dtype=jnp.int32))
    summed = jax.ops.segment_sum(partial_rows.reshape(BLOCKS, NF), component, NCOMP)
    diag_sum = jax.ops.segment_sum(diag_rows.reshape(BLOCKS), component, NCOMP)
    traces_new = jnp.maximum(0.0, previous + summed.T / (diag_sum + 1.0)[None, :])
    new_bf = traces_new.astype(jnp.bfloat16)

    def brick_update(brick_index):
        slab_data = lax.dynamic_index_in_dim(slabs, brick_index, 1, keepdims=False)
        foot = foot_grid[brick_index].astype(jnp.float32)
        slot_new = jnp.take(new_bf, comp_grid[brick_index], axis=1)
        product = jnp.dot(slot_new.T, slab_data, preferred_element_type=jnp.float32)
        slot_wide = slot_new.astype(jnp.float32)
        gram = jnp.dot(slot_wide.T, slot_wide, precision=lax.Precision.HIGHEST)
        gradient = product - jnp.dot(gram, foot, precision=lax.Precision.HIGHEST)
        denominator = jnp.diagonal(gram) + 1.0
        stepped = jnp.where(foot > 0, jnp.maximum(foot + gradient / denominator[:, None], 0.0), 0.0)
        return stepped.astype(jnp.bfloat16)

    footprints_new = lax.map(brick_update, jnp.arange(N_BRICKS, dtype=jnp.int32)).reshape(BLOCKS, V_DEV)
    return traces_new, footprints_new
```

```python
import functools

import jax
import jax.numpy as jnp
from jax import lax
from jax.experimental import pallas as pl
from jax.experimental.pallas import tpu as pltpu
from jax.sharding import PartitionSpec as P

TIME_STEP = 0.14
SWEEPS = 3
LANES = 128
HIGHEST = lax.Precision.HIGHEST
MESH = pl.DeviceIdType.MESH
VMEM = pl.BlockSpec(memory_space=pltpu.VMEM)
SMEM = pl.BlockSpec(memory_space=pltpu.SMEM)


def meet(axes):
    barrier = pltpu.get_barrier_semaphore()
    total = 0
    for axis in axes:
        count = lax.axis_size(axis)
        me = lax.axis_index(axis)

        def tell(d, carry, axis=axis, count=count, me=me):
            pl.semaphore_signal(
                barrier, inc=1, device_id={axis: lax.rem(me + d, count)}, device_id_type=MESH
            )
            return carry

        lax.fori_loop(1, count, tell, 0)
        total += count - 1
    pl.semaphore_wait(barrier, total)


def share_copy(axis, gathered, source, send, recv, d):
    count = lax.axis_size(axis)
    me = lax.axis_index(axis)
    return pltpu.make_async_remote_copy(
        src_ref=source,
        dst_ref=gathered.at[me],
        send_sem=send.at[d],
        recv_sem=recv.at[d],
        device_id={axis: lax.rem(me + d, count)},
        device_id_type=MESH,
    )


def share_start(axis, gathered, source, send, recv):
    def go(d, carry):
        share_copy(axis, gathered, source, send, recv, d).start()
        return carry

    lax.fori_loop(1, lax.axis_size(axis), go, 0)


def share_wait(axis, gathered, source, send, recv):
    def go(d, carry):
        share_copy(axis, gathered, source, send, recv, d).wait()
        return carry

    lax.fori_loop(1, lax.axis_size(axis), go, 0)


def first_exchange(rec, info, low, high, infos, hsend, hrecv, send, recv):
    n = lax.axis_size("bricks")
    me = lax.axis_index("bricks")
    planes = rec.shape[0]
    meet(("bricks",))
    to_right = pltpu.make_async_remote_copy(
        src_ref=rec.at[pl.ds(planes - SWEEPS, SWEEPS)],
        dst_ref=low,
        send_sem=hsend.at[0],
        recv_sem=hrecv.at[0],
        device_id={"bricks": lax.rem(me + 1, n)},
        device_id_type=MESH,
    )
    to_left = pltpu.make_async_remote_copy(
        src_ref=rec.at[pl.ds(0, SWEEPS)],
        dst_ref=high,
        send_sem=hsend.at[1],
        recv_sem=hrecv.at[1],
        device_id={"bricks": lax.rem(me + n - 1, n)},
        device_id_type=MESH,
    )

    @pl.when(me < n - 1)
    def _():
        to_right.start()

    @pl.when(me > 0)
    def _():
        to_left.start()

    share_start("bricks", infos, info, send, recv)
    infos[me] = info[...]

    @pl.when(me == 0)
    def _():
        low[...] = jnp.zeros_like(low)

    @pl.when(me == n - 1)
    def _():
        high[...] = jnp.zeros_like(high)

    share_wait("bricks", infos, info, send, recv)

    @pl.when(me < n - 1)
    def _():
        to_right.wait_send()
        to_left.wait_recv()

    @pl.when(me > 0)
    def _():
        to_left.wait_send()
        to_right.wait_recv()


def flux_of(difference):
    below = 1.0 + difference * difference
    near = pl.reciprocal(below, approx=True)
    return difference * (near * (2.0 - below * near))


def sweep(load, store, planes, rows, shape):
    lane = lax.broadcasted_iota(jnp.int32, shape, 1)
    width = shape[1]

    def row(z, fluxes):
        out = []
        center = load(1, z)
        flux_x = flux_of(center - load(0, z))
        for x in range(planes):
            right = load(x + 2, z)
            next_x = flux_of(right - center)
            ahead = load(x + 1, jnp.minimum(z + 1, rows - 1))
            ahead = jnp.where(z + 1 < rows, ahead, 0.0)
            next_z = flux_of(ahead - center)
            beside = jnp.where(lane == width - 1, 0.0, pltpu.roll(center, width - 1, 1))
            next_y = flux_of(beside - center)
            edge = flux_of(center[:, :LANES])
            edge = jnp.concatenate([edge, jnp.zeros((shape[0], width - LANES), jnp.float32)], axis=1)
            prev_y = jnp.where(lane == 0, edge, pltpu.roll(next_y, 1, 1))
            total = (next_x - flux_x) + (next_z - fluxes[x]) + (next_y - prev_y)
            store(x, z, center + TIME_STEP * total)
            out.append(next_z)
            flux_x = next_x
            center = right
        return tuple(out)

    first = tuple(flux_of(load(x + 1, 0)) for x in range(planes))
    lax.fori_loop(0, rows, row, first)


def local_kernel(
    tiles, at, rec, low, high, foot, slot_traces, message, windows, own, one, two, y_tiles, zero
):
    n = lax.axis_size("bricks")
    me = lax.axis_index("bricks")
    planes, rows, frames, width = rec.shape
    slots = foot.shape[0]
    shape = (frames, width)
    per = width // LANES

    def load_first(x, z):
        if x < SWEEPS:
            return low[x, z].astype(jnp.float32)
        if x < SWEEPS + planes:
            return rec[x - SWEEPS, z].astype(jnp.float32)
        return high[x - SWEEPS - planes, z].astype(jnp.float32)

    def keep(ref, margin):
        def store(x, z, value):
            if x < margin:
                value = jnp.where(me > 0, value, 0.0)
            if x >= planes + margin:
                value = jnp.where(me < n - 1, value, 0.0)
            ref[x, z] = value

        return store

    def store_last(x, z, value):
        value = value.astype(jnp.bfloat16)
        for h in range(per):
            y_tiles[(x * rows + z) * per + h] = value[:, h * LANES : (h + 1) * LANES]

    sweep(load_first, keep(one, 2), planes + 4, rows, shape)
    sweep(lambda x, z: one[x, z], keep(two, 1), planes + 2, rows, shape)
    sweep(lambda x, z: two[x, z], store_last, planes, rows, shape)

    sub = lax.broadcasted_iota(jnp.int32, (slots, 2 * LANES), 0)
    mine = jnp.zeros((slots, 2 * LANES), jnp.float32)
    for k in range(slots):
        t = at[k]
        u = lax.rem(t + 1, tiles)
        rows_a = jnp.concatenate(
            [
                foot[:, pl.ds(pl.multiple_of(t * LANES, LANES), LANES)],
                foot[:, pl.ds(pl.multiple_of(u * LANES, LANES), LANES)],
            ],
            axis=1,
        )
        windows[k, frames:, :] = rows_a
        windows[k, :frames, :] = jnp.concatenate([y_tiles[t], y_tiles[u]], axis=1)
        mine = jnp.where(sub == k, rows_a.astype(jnp.float32), mine)
    own[...] = mine
    mine_bf = mine.astype(jnp.bfloat16)
    wide = frames + slots
    sub = lax.broadcasted_iota(jnp.int32, (slots, wide), 0)
    both = jnp.zeros((slots, wide), jnp.float32)
    for k in range(slots):
        found = lax.dot_general(
            mine_bf, windows[k], (((1,), (1,)), ((), ())), preferred_element_type=jnp.float32
        )
        both = jnp.where(sub == k, found, both)
    correlation = both[:, frames:]
    removed = jnp.dot(correlation, slot_traces[...], precision=HIGHEST)
    eye = lax.broadcasted_iota(jnp.int32, (slots, slots), 0) == lax.broadcasted_iota(
        jnp.int32, (slots, slots), 1
    )
    diag = jnp.sum(jnp.where(eye, correlation, 0.0), axis=1, keepdims=True)
    lane = lax.broadcasted_iota(jnp.int32, (slots, LANES), 1)
    wide_value = jnp.concatenate(
        [both[:, :frames], jnp.zeros((slots, LANES - frames), jnp.float32)], axis=1
    )
    message[...] = jnp.where(lane == frames, diag, wide_value - removed)


def split3(value):
    a = value.astype(jnp.bfloat16)
    rest = value - a.astype(jnp.float32)
    b = rest.astype(jnp.bfloat16)
    c = (rest - b.astype(jnp.float32)).astype(jnp.bfloat16)
    return a, b, c


def second_exchange(
    frames, message, same, prior, windows, own, new_out, result,
    gathered, grad, grads, send, recv, gsend, grecv,
):
    n = lax.axis_size("bricks")
    me = lax.axis_index("bricks")
    groups = lax.axis_size("frames")
    slots = own.shape[0]
    meet(("bricks", "frames"))
    share_start("bricks", gathered, message, send, recv)
    gathered[me] = message[...]
    share_wait("bricks", gathered, message, send, recv)
    everything = gathered[...].reshape(n * slots, LANES)
    parts = jnp.concatenate(split3(everything), axis=1)
    found = jnp.dot(same[...], parts, preferred_element_type=jnp.float32)
    summed = found[:, :LANES] + found[:, LANES : 2 * LANES] + found[:, 2 * LANES :]
    diag = summed[:, frames : frames + 1]
    new = jnp.maximum(0.0, prior[...] + summed / (diag + 1.0))
    new_out[...] = new[slots:, :frames]
    picked = new[:slots, :frames].astype(jnp.bfloat16)
    gram = lax.dot_general(
        picked, picked, (((1,), (1,)), ((), ())), preferred_element_type=jnp.float32
    )
    g1, g2, g3 = split3(gram)
    none = jnp.zeros((slots, frames), jnp.float32)
    left = jnp.concatenate(
        [
            jnp.concatenate([picked.astype(jnp.float32), -g1.astype(jnp.float32)], axis=1),
            jnp.concatenate([none, -g2.astype(jnp.float32)], axis=1),
            jnp.concatenate([none, -g3.astype(jnp.float32)], axis=1),
        ],
        axis=0,
    ).astype(jnp.bfloat16)
    sub = lax.broadcasted_iota(jnp.int32, (slots, 2 * LANES), 0)
    total = jnp.zeros((slots, 2 * LANES), jnp.float32)
    for k in range(slots):
        one = jnp.dot(left, windows[k], preferred_element_type=jnp.float32)
        one = one[:slots] + one[slots : 2 * slots] + one[2 * slots :]
        total = jnp.where(sub == k, one, total)
    eye = lax.broadcasted_iota(jnp.int32, (slots, slots), 0) == lax.broadcasted_iota(
        jnp.int32, (slots, slots), 1
    )
    gdiag = jnp.sum(jnp.where(eye, gram, 0.0), axis=1, keepdims=True)
    grad[:, : 2 * LANES] = total
    grad[:, 2 * LANES :] = jnp.broadcast_to(gdiag, (slots, LANES))
    share_start("frames", grads, grad, gsend, grecv)
    grads[lax.axis_index("frames")] = grad[...]
    share_wait("frames", grads, grad, gsend, grecv)
    whole = grads[0]
    for g in range(1, groups):
        whole = whole + grads[g]
    current = own[...]
    step = whole[:, : 2 * LANES] / (whole[:, 2 * LANES : 2 * LANES + 1] + 1.0)
    result[...] = jnp.where(current > 0, jnp.maximum(current + step, 0.0), 0.0)


def spread_kernel(tiles, at, result, out):
    slots = out.shape[0]
    first = jnp.broadcast_to(at[...], (slots, LANES))
    second = jnp.where(first + 1 == tiles, 0, first + 1)
    head = result[:, :LANES]
    tail = result[:, LANES:]
    for t in range(tiles):
        out[:, t * LANES : (t + 1) * LANES] = jnp.where(
            first == t, head, jnp.where(second == t, tail, 0.0)
        ).astype(jnp.bfloat16)


def shards(recording, traces, footprints, block_owner, block_slot):
    frames, planes, rows, width = recording.shape
    slots, voxels = footprints.shape
    owned = traces.shape[1]
    n = lax.axis_size("bricks")
    groups = lax.axis_size("frames")
    me = lax.axis_index("bricks")
    tiles = voxels // LANES
    f32 = jnp.float32
    sds = jax.ShapeDtypeStruct
    dma = pltpu.SemaphoreType.DMA
    component = block_owner[:, 0] * owned + block_slot
    rec = jnp.transpose(recording, (1, 2, 0, 3))
    info = jnp.concatenate([traces.T.astype(f32), component.astype(f32)[:, None]], axis=1)

    low, high, infos = pl.pallas_call(
        first_exchange,
        out_shape=(
            sds((SWEEPS, rows, frames, width), jnp.bfloat16),
            sds((SWEEPS, rows, frames, width), jnp.bfloat16),
            sds((n,) + info.shape, f32),
        ),
        in_specs=[VMEM, VMEM],
        out_specs=(VMEM, VMEM, VMEM),
        scratch_shapes=[dma((2,)), dma((2,)), dma((n,)), dma((n,))],
        compiler_params=pltpu.CompilerParams(
            collective_id=0, has_side_effects=True, vmem_limit_bytes=16 << 20
        ),
        name="first_exchange",
    )(rec, info)

    positive = jnp.any((footprints > 0).reshape(slots, tiles, LANES), axis=2)
    begins = positive & ~jnp.roll(positive, 1, axis=1)
    at = jnp.sum(jnp.where(begins, jnp.arange(tiles, dtype=jnp.int32)[None, :], 0), axis=1)

    infos = infos.reshape(n * slots, frames + 1)
    everyone = infos[:, frames].astype(jnp.int32)
    wanted = jnp.concatenate([component, me * owned + jnp.arange(owned, dtype=jnp.int32)])
    same = (wanted[:, None] == everyone[None, :]).astype(jnp.bfloat16)
    picks = (component[:, None] == jnp.arange(n * owned, dtype=jnp.int32)[None, :]).astype(
        jnp.bfloat16
    )
    slot_traces = jnp.dot(
        picks, infos[:, :frames].astype(jnp.bfloat16), preferred_element_type=f32
    )
    prior = jnp.pad(
        jnp.concatenate([slot_traces, traces.T.astype(f32)], axis=0),
        ((0, 0), (0, LANES - frames)),
    )

    message, windows, own = pl.pallas_call(
        functools.partial(local_kernel, tiles),
        out_shape=(
            sds((slots, LANES), f32),
            sds((slots, frames + slots, 2 * LANES), jnp.bfloat16),
            sds((slots, 2 * LANES), f32),
        ),
        in_specs=[SMEM, VMEM, VMEM, VMEM, VMEM, VMEM],
        out_specs=(VMEM, VMEM, VMEM),
        scratch_shapes=[
            pltpu.VMEM((planes + 4, rows, frames, width), f32),
            pltpu.VMEM((planes + 2, rows, frames, width), f32),
            pltpu.VMEM((tiles, frames, LANES), jnp.bfloat16),
            pltpu.VMEM((8, LANES), f32),
        ],
        compiler_params=pltpu.CompilerParams(vmem_limit_bytes=32 << 20),
        name="denoise_project",
    )(at, rec, low, high, footprints, prior[:slots])

    new_t, result = pl.pallas_call(
        functools.partial(second_exchange, frames),
        out_shape=(sds((owned, frames), f32), sds((slots, 2 * LANES), f32)),
        in_specs=[VMEM] * 5,
        out_specs=(VMEM, VMEM),
        scratch_shapes=[
            pltpu.VMEM((n, slots, LANES), f32),
            pltpu.VMEM((slots, 3 * LANES), f32),
            pltpu.VMEM((groups, slots, 3 * LANES), f32),
            dma((n,)),
            dma((n,)),
            dma((groups,)),
            dma((groups,)),
        ],
        compiler_params=pltpu.CompilerParams(
            collective_id=1, has_side_effects=True, vmem_limit_bytes=16 << 20
        ),
        name="second_exchange",
    )(message, same, prior, windows, own)

    footprints_new = pl.pallas_call(
        functools.partial(spread_kernel, tiles),
        out_shape=sds((slots, voxels), jnp.bfloat16),
        in_specs=[VMEM, VMEM],
        out_specs=VMEM,
        name="spread",
    )(at[:, None], result)
    return (new_t.T, footprints_new)


def solution(mesh):
    return jax.shard_map(
        shards,
        mesh=mesh,
        in_specs=(
            P("frames", "bricks", None, None),
            P("frames", "bricks"),
            P("bricks", None),
            P("bricks", None),
            P("bricks"),
        ),
        out_specs=(P("frames", "bricks"), P("bricks", None)),
        check_vma=False,
    )
```

```python
import functools

import jax
import jax.numpy as jnp
from jax import lax
from jax.experimental import pallas as pl
from jax.experimental.pallas import tpu as pltpu
from jax.sharding import PartitionSpec as P

TIME_STEP = 0.14
SWEEPS = 3
LANES = 128
HIGHEST = lax.Precision.HIGHEST
MESH = pl.DeviceIdType.MESH
VMEM = pl.BlockSpec(memory_space=pltpu.VMEM)
SMEM = pl.BlockSpec(memory_space=pltpu.SMEM)


def meet(axes):
    barrier = pltpu.get_barrier_semaphore()
    total = 0
    for axis in axes:
        count = lax.axis_size(axis)
        me = lax.axis_index(axis)

        def tell(d, carry, axis=axis, count=count, me=me):
            pl.semaphore_signal(
                barrier, inc=1, device_id={axis: lax.rem(me + d, count)}, device_id_type=MESH
            )
            return carry

        lax.fori_loop(1, count, tell, 0)
        total += count - 1
    pl.semaphore_wait(barrier, total)


def share_copy(axis, gathered, source, send, recv, d):
    count = lax.axis_size(axis)
    me = lax.axis_index(axis)
    return pltpu.make_async_remote_copy(
        src_ref=source,
        dst_ref=gathered.at[me],
        send_sem=send.at[d],
        recv_sem=recv.at[d],
        device_id={axis: lax.rem(me + d, count)},
        device_id_type=MESH,
    )


def share_start(axis, gathered, source, send, recv):
    def go(d, carry):
        share_copy(axis, gathered, source, send, recv, d).start()
        return carry

    lax.fori_loop(1, lax.axis_size(axis), go, 0)


def share_wait(axis, gathered, source, send, recv):
    def go(d, carry):
        share_copy(axis, gathered, source, send, recv, d).wait()
        return carry

    lax.fori_loop(1, lax.axis_size(axis), go, 0)


def first_exchange(rec, info, low, high, infos, hsend, hrecv, send, recv):
    n = lax.axis_size("bricks")
    me = lax.axis_index("bricks")
    planes = rec.shape[0]
    meet(("bricks",))
    to_right = pltpu.make_async_remote_copy(
        src_ref=rec.at[pl.ds(planes - SWEEPS, SWEEPS)],
        dst_ref=low,
        send_sem=hsend.at[0],
        recv_sem=hrecv.at[0],
        device_id={"bricks": lax.rem(me + 1, n)},
        device_id_type=MESH,
    )
    to_left = pltpu.make_async_remote_copy(
        src_ref=rec.at[pl.ds(0, SWEEPS)],
        dst_ref=high,
        send_sem=hsend.at[1],
        recv_sem=hrecv.at[1],
        device_id={"bricks": lax.rem(me + n - 1, n)},
        device_id_type=MESH,
    )

    @pl.when(me < n - 1)
    def _():
        to_right.start()

    @pl.when(me > 0)
    def _():
        to_left.start()

    share_start("bricks", infos, info, send, recv)
    infos[me] = info[...]

    @pl.when(me == 0)
    def _():
        low[...] = jnp.zeros_like(low)

    @pl.when(me == n - 1)
    def _():
        high[...] = jnp.zeros_like(high)

    share_wait("bricks", infos, info, send, recv)

    @pl.when(me < n - 1)
    def _():
        to_right.wait_send()
        to_left.wait_recv()

    @pl.when(me > 0)
    def _():
        to_left.wait_send()
        to_right.wait_recv()


def flux_of(difference):
    below = 1.0 + difference * difference
    near = pl.reciprocal(below, approx=True)
    return difference * (near * (2.0 - below * near))


def sweep(load, store, planes, rows, shape):
    lane = lax.broadcasted_iota(jnp.int32, shape, 1)
    width = shape[1]

    def row(z, fluxes):
        out = []
        center = load(1, z)
        flux_x = flux_of(center - load(0, z))
        for x in range(planes):
            right = load(x + 2, z)
            next_x = flux_of(right - center)
            ahead = load(x + 1, jnp.minimum(z + 1, rows - 1))
            ahead = jnp.where(z + 1 < rows, ahead, 0.0)
            next_z = flux_of(ahead - center)
            beside = jnp.where(lane == width - 1, 0.0, pltpu.roll(center, width - 1, 1))
            next_y = flux_of(beside - center)
            edge = flux_of(center[:, :LANES])
            edge = jnp.concatenate([edge, jnp.zeros((shape[0], width - LANES), jnp.float32)], axis=1)
            prev_y = jnp.where(lane == 0, edge, pltpu.roll(next_y, 1, 1))
            total = (next_x - flux_x) + (next_z - fluxes[x]) + (next_y - prev_y)
            store(x, z, center + TIME_STEP * total)
            out.append(next_z)
            flux_x = next_x
            center = right
        return tuple(out)

    first = tuple(flux_of(load(x + 1, 0)) for x in range(planes))
    lax.fori_loop(0, rows, row, first)


def side_by_side(ref):
    return jnp.concatenate([ref[s] for s in range(ref.shape[0])], axis=1)


def unpacked(packed, frames, groups):
    count = frames // groups
    width = packed.shape[1] // groups
    cuts = [packed[:count, g * width : (g + 1) * width] for g in range(groups)]
    return jnp.concatenate(cuts, axis=0), packed[count : count + 1, :width]


def local_kernel(
    tiles, at, rec, low, high, foot, infos, picks, message, windows, own, slot_traces, one, two, y_tiles
):
    n = lax.axis_size("bricks")
    me = lax.axis_index("bricks")
    planes, rows, frames, width = rec.shape
    slots = foot.shape[0]
    shape = (frames, width)
    per = width // LANES

    def load_first(x, z):
        if x < SWEEPS:
            return low[x, z].astype(jnp.float32)
        if x < SWEEPS + planes:
            return rec[x - SWEEPS, z].astype(jnp.float32)
        return high[x - SWEEPS - planes, z].astype(jnp.float32)

    def keep(ref, margin):
        def store(x, z, value):
            if x < margin:
                value = jnp.where(me > 0, value, 0.0)
            if x >= planes + margin:
                value = jnp.where(me < n - 1, value, 0.0)
            ref[x, z] = value

        return store

    def store_last(x, z, value):
        value = value.astype(jnp.bfloat16)
        for h in range(per):
            y_tiles[(x * rows + z) * per + h] = value[:, h * LANES : (h + 1) * LANES]

    sweep(load_first, keep(one, 2), planes + 4, rows, shape)
    sweep(lambda x, z: one[x, z], keep(two, 1), planes + 2, rows, shape)
    sweep(lambda x, z: two[x, z], store_last, planes, rows, shape)

    sub = lax.broadcasted_iota(jnp.int32, (slots, 2 * LANES), 0)
    mine = jnp.zeros((slots, 2 * LANES), jnp.float32)
    for k in range(slots):
        t = at[k, 0]
        u = lax.rem(t + 1, tiles)
        rows_a = jnp.concatenate(
            [
                foot[:, pl.ds(pl.multiple_of(t * LANES, LANES), LANES)],
                foot[:, pl.ds(pl.multiple_of(u * LANES, LANES), LANES)],
            ],
            axis=1,
        )
        windows[k, frames:, :] = rows_a
        windows[k, :frames, :] = jnp.concatenate([y_tiles[t], y_tiles[u]], axis=1)
        mine = jnp.where(sub == k, rows_a.astype(jnp.float32), mine)
    own[...] = mine
    mine_bf = mine.astype(jnp.bfloat16)
    wide = frames + slots
    lane = lax.broadcasted_iota(jnp.int32, (wide, slots), 1)
    both = jnp.zeros((wide, slots), jnp.float32)
    for k in range(slots):
        found = lax.dot_general(
            windows[k], mine_bf, (((1,), (1,)), ((), ())), preferred_element_type=jnp.float32
        )
        both = jnp.where(lane == k, found, both)
    correlation = both[frames:]
    groups = LANES // slots
    count = frames // groups
    prior = jnp.dot(
        side_by_side(infos).astype(jnp.bfloat16), picks[...], preferred_element_type=jnp.float32
    )
    prior, _ = unpacked(prior, frames, groups)
    slot_traces[...] = prior
    partial = both[:frames] - jnp.dot(prior, correlation, precision=HIGHEST)
    eye = lax.broadcasted_iota(jnp.int32, (slots, slots), 0) == lax.broadcasted_iota(
        jnp.int32, (slots, slots), 1
    )
    diag = jnp.sum(jnp.where(eye, correlation, 0.0), axis=0, keepdims=True)
    message[...] = jnp.zeros_like(message)
    for g in range(groups):
        message[:count, g * slots : (g + 1) * slots] = partial[g * count : (g + 1) * count]
    message[count : count + 1, :slots] = diag


def split3(value):
    a = value.astype(jnp.bfloat16)
    rest = value - a.astype(jnp.float32)
    b = rest.astype(jnp.bfloat16)
    c = (rest - b.astype(jnp.float32)).astype(jnp.bfloat16)
    return a, b, c


def second_exchange(
    frames, message, same, prior, windows, own, new_out, result,
    gathered, grad, grads, send, recv, gsend, grecv,
):
    n = lax.axis_size("bricks")
    me = lax.axis_index("bricks")
    groups = lax.axis_size("frames")
    slots = own.shape[0]
    meet(("bricks", "frames"))
    share_start("bricks", gathered, message, send, recv)
    gathered[me] = message[...]
    share_wait("bricks", gathered, message, send, recv)
    parts = [part.astype(jnp.float32) for part in split3(side_by_side(gathered))]
    parts = jnp.concatenate(parts, axis=0).astype(jnp.bfloat16)
    found = jnp.dot(parts, same[...], preferred_element_type=jnp.float32)
    high = message.shape[0]
    found = found[:high] + found[high : 2 * high] + found[2 * high :]
    summed, diag = unpacked(found, frames, LANES // slots)
    new = jnp.maximum(0.0, prior[...] + summed / (diag + 1.0))
    new_out[...] = new[:, slots:]
    turn = lax.broadcasted_iota(jnp.int32, (slots, slots), 0) == lax.broadcasted_iota(
        jnp.int32, (slots, slots), 1
    )
    picked = lax.dot_general(
        jnp.where(turn, 1.0, 0.0).astype(jnp.bfloat16),
        new[:, :slots].astype(jnp.bfloat16),
        (((1,), (1,)), ((), ())),
        preferred_element_type=jnp.float32,
    ).astype(jnp.bfloat16)
    gram = lax.dot_general(
        picked, picked, (((1,), (1,)), ((), ())), preferred_element_type=jnp.float32
    )
    g1, g2, g3 = split3(gram)
    none = jnp.zeros((slots, frames), jnp.float32)
    left = jnp.concatenate(
        [
            jnp.concatenate([picked.astype(jnp.float32), -g1.astype(jnp.float32)], axis=1),
            jnp.concatenate([none, -g2.astype(jnp.float32)], axis=1),
            jnp.concatenate([none, -g3.astype(jnp.float32)], axis=1),
        ],
        axis=0,
    ).astype(jnp.bfloat16)
    sub = lax.broadcasted_iota(jnp.int32, (slots, 2 * LANES), 0)
    total = jnp.zeros((slots, 2 * LANES), jnp.float32)
    for k in range(slots):
        one = jnp.dot(left, windows[k], preferred_element_type=jnp.float32)
        one = one[:slots] + one[slots : 2 * slots] + one[2 * slots :]
        total = jnp.where(sub == k, one, total)
    eye = lax.broadcasted_iota(jnp.int32, (slots, slots), 0) == lax.broadcasted_iota(
        jnp.int32, (slots, slots), 1
    )
    gdiag = jnp.sum(jnp.where(eye, gram, 0.0), axis=1, keepdims=True)
    grad[:, : 2 * LANES] = total
    grad[:, 2 * LANES :] = jnp.broadcast_to(gdiag, (slots, LANES))
    share_start("frames", grads, grad, gsend, grecv)
    grads[lax.axis_index("frames")] = grad[...]
    share_wait("frames", grads, grad, gsend, grecv)
    whole = grads[0]
    for g in range(1, groups):
        whole = whole + grads[g]
    current = own[...]
    step = whole[:, : 2 * LANES] / (whole[:, 2 * LANES : 2 * LANES + 1] + 1.0)
    result[...] = jnp.where(current > 0, jnp.maximum(current + step, 0.0), 0.0)


def find_kernel(tiles, foot, at):
    where = jnp.zeros((foot.shape[0], LANES), jnp.int32)
    for t in range(tiles):
        cut = foot[:, t * LANES : (t + 1) * LANES].astype(jnp.float32)
        where = jnp.where(cut > 0, t, where)
    at[...] = jnp.broadcast_to(where[:, LANES - 1 :], where.shape)


def spread_kernel(tiles, at, result, new, out, new_out):
    slots, width = out.shape
    base = pl.program_id(0) * (width // LANES)
    first = at[...] - base
    second = jnp.where(at[...] + 1 == tiles, 0, at[...] + 1) - base
    head = result[:, :LANES]
    tail = result[:, LANES:]
    for t in range(width // LANES):
        out[:, t * LANES : (t + 1) * LANES] = jnp.where(
            first == t, head, jnp.where(second == t, tail, 0.0)
        ).astype(jnp.bfloat16)
    new_out[...] = new[...]


def spread_groups(matches, groups):
    n, k, m = matches.shape
    eye = jnp.arange(groups)[:, None] == jnp.arange(groups)[None, :]
    out = matches[:, None, :, None, :] & eye[None, :, None, :, None]
    return out.reshape(n * groups * k, groups * m).astype(jnp.bfloat16)


def shards(recording, traces, footprints, block_owner, block_slot):
    frames, planes, rows, width = recording.shape
    slots, voxels = footprints.shape
    owned = traces.shape[1]
    n = lax.axis_size("bricks")
    groups = lax.axis_size("frames")
    me = lax.axis_index("bricks")
    tiles = voxels // LANES
    f32 = jnp.float32
    sds = jax.ShapeDtypeStruct
    dma = pltpu.SemaphoreType.DMA
    component = block_owner[:, 0] * owned + block_slot
    rec = jnp.transpose(recording, (1, 2, 0, 3))
    packs = LANES // slots
    count = frames // packs
    high_rows = -(-(count + 1) // 8) * 8
    info = traces.astype(f32).reshape(packs, count, owned).transpose(1, 0, 2).reshape(count, LANES)
    extra = jnp.pad(component.astype(f32)[None, :], ((0, high_rows - count - 1), (0, LANES - slots)))
    info = jnp.concatenate([info, extra], axis=0)
    at = pl.pallas_call(
        functools.partial(find_kernel, tiles),
        out_shape=sds((slots, LANES), jnp.int32),
        in_specs=[VMEM],
        out_specs=VMEM,
        name="find",
    )(footprints)
    places = jnp.arange(n * owned, dtype=jnp.int32).reshape(n, owned)
    picks = spread_groups(places[:, :, None] == component[None, None, :], packs)

    low, high, infos = pl.pallas_call(
        first_exchange,
        out_shape=(
            sds((SWEEPS, rows, frames, width), jnp.bfloat16),
            sds((SWEEPS, rows, frames, width), jnp.bfloat16),
            sds((n,) + info.shape, f32),
        ),
        in_specs=[VMEM, VMEM],
        out_specs=(VMEM, VMEM, VMEM),
        scratch_shapes=[dma((2,)), dma((2,)), dma((n,)), dma((n,))],
        compiler_params=pltpu.CompilerParams(
            collective_id=0, has_side_effects=True, vmem_limit_bytes=16 << 20
        ),
        name="first_exchange",
    )(rec, info)

    message, windows, own, slot_traces = pl.pallas_call(
        functools.partial(local_kernel, tiles),
        out_shape=(
            sds((high_rows, LANES), f32),
            sds((slots, frames + slots, 2 * LANES), jnp.bfloat16),
            sds((slots, 2 * LANES), f32),
            sds((frames, slots), f32),
        ),
        in_specs=[SMEM] + [VMEM] * 6,
        out_specs=(VMEM,) * 4,
        scratch_shapes=[
            pltpu.VMEM((planes + 4, rows, frames, width), f32),
            pltpu.VMEM((planes + 2, rows, frames, width), f32),
            pltpu.VMEM((tiles, frames, LANES), jnp.bfloat16),
        ],
        compiler_params=pltpu.CompilerParams(vmem_limit_bytes=32 << 20),
        name="denoise_project",
    )(at, rec, low, high, footprints, infos, picks)

    everyone = infos[:, count, :slots].astype(jnp.int32)
    wanted = jnp.concatenate([component, me * owned + jnp.arange(owned, dtype=jnp.int32)])
    same = spread_groups(everyone[:, :, None] == wanted[None, None, :], packs)
    prior = jnp.concatenate([slot_traces, traces.astype(f32)], axis=1)

    new, result = pl.pallas_call(
        functools.partial(second_exchange, frames),
        out_shape=(sds((frames, owned), f32), sds((slots, 2 * LANES), f32)),
        in_specs=[VMEM] * 5,
        out_specs=(VMEM, VMEM),
        scratch_shapes=[
            pltpu.VMEM((n, high_rows, LANES), f32),
            pltpu.VMEM((slots, 3 * LANES), f32),
            pltpu.VMEM((groups, slots, 3 * LANES), f32),
            dma((n,)),
            dma((n,)),
            dma((groups,)),
            dma((groups,)),
        ],
        compiler_params=pltpu.CompilerParams(
            collective_id=1, has_side_effects=True, vmem_limit_bytes=16 << 20
        ),
        name="second_exchange",
    )(message, same, prior, windows, own)

    steps = 4 if tiles % 4 == 0 else 1
    footprints_new, traces_new = pl.pallas_call(
        functools.partial(spread_kernel, tiles),
        out_shape=(sds((slots, voxels), jnp.bfloat16), sds((frames, owned), f32)),
        grid=(steps,),
        in_specs=[
            pl.BlockSpec((slots, LANES), lambda i: (0, 0)),
            pl.BlockSpec((slots, 2 * LANES), lambda i: (0, 0)),
            pl.BlockSpec((frames, owned), lambda i: (0, 0)),
        ],
        out_specs=(
            pl.BlockSpec((slots, voxels // steps), lambda i: (0, i)),
            pl.BlockSpec((frames, owned), lambda i: (0, 0)),
        ),
        name="spread",
    )(at, result, new)
    return (traces_new, footprints_new)


def solution(mesh):
    return jax.shard_map(
        shards,
        mesh=mesh,
        in_specs=(
            P("frames", "bricks", None, None),
            P("frames", "bricks"),
            P("bricks", None),
            P("bricks", None),
            P("bricks"),
        ),
        out_specs=(P("frames", "bricks"), P("bricks", None)),
        check_vma=False,
    )
```

```python
import functools

import jax
import jax.numpy as jnp
from jax import lax
from jax.experimental import pallas as pl
from jax.experimental.pallas import tpu as pltpu
from jax.sharding import PartitionSpec as P

TIME_STEP = 0.14
SWEEPS = 3
LANES = 128
HIGHEST = lax.Precision.HIGHEST
MESH = pl.DeviceIdType.MESH
VMEM = pl.BlockSpec(memory_space=pltpu.VMEM)
SMEM = pl.BlockSpec(memory_space=pltpu.SMEM)


def meet(axes):
    barrier = pltpu.get_barrier_semaphore()
    total = 0
    for axis in axes:
        count = lax.axis_size(axis)
        me = lax.axis_index(axis)

        def tell(d, carry, axis=axis, count=count, me=me):
            pl.semaphore_signal(
                barrier, inc=1, device_id={axis: lax.rem(me + d, count)}, device_id_type=MESH
            )
            return carry

        lax.fori_loop(1, count, tell, 0)
        total += count - 1
    pl.semaphore_wait(barrier, total)


def share_copy(axis, gathered, source, send, recv, d):
    count = lax.axis_size(axis)
    me = lax.axis_index(axis)
    return pltpu.make_async_remote_copy(
        src_ref=source,
        dst_ref=gathered.at[me],
        send_sem=send.at[d],
        recv_sem=recv.at[d],
        device_id={axis: lax.rem(me + d, count)},
        device_id_type=MESH,
    )


def share_start(axis, gathered, source, send, recv):
    def go(d, carry):
        share_copy(axis, gathered, source, send, recv, d).start()
        return carry

    lax.fori_loop(1, lax.axis_size(axis), go, 0)


def share_wait(axis, gathered, source, send, recv):
    def go(d, carry):
        share_copy(axis, gathered, source, send, recv, d).wait()
        return carry

    lax.fori_loop(1, lax.axis_size(axis), go, 0)


def find_first(foot, at):
    tiles = foot.shape[1] // LANES
    where = jnp.zeros((foot.shape[0], LANES), jnp.int32)
    for t in range(tiles):
        cut = foot[:, t * LANES : (t + 1) * LANES].astype(jnp.float32)
        where = jnp.where(cut > 0, t, where)
    at[...] = jnp.broadcast_to(where[:, LANES - 1 :], where.shape)


def first_exchange(rec, info, foot, low, high, infos, at, hsend, hrecv, send, recv):
    n = lax.axis_size("bricks")
    me = lax.axis_index("bricks")
    planes = rec.shape[0]
    meet(("bricks",))
    to_right = pltpu.make_async_remote_copy(
        src_ref=rec.at[pl.ds(planes - SWEEPS, SWEEPS)],
        dst_ref=low,
        send_sem=hsend.at[0],
        recv_sem=hrecv.at[0],
        device_id={"bricks": lax.rem(me + 1, n)},
        device_id_type=MESH,
    )
    to_left = pltpu.make_async_remote_copy(
        src_ref=rec.at[pl.ds(0, SWEEPS)],
        dst_ref=high,
        send_sem=hsend.at[1],
        recv_sem=hrecv.at[1],
        device_id={"bricks": lax.rem(me + n - 1, n)},
        device_id_type=MESH,
    )

    @pl.when(me < n - 1)
    def _():
        to_right.start()

    @pl.when(me > 0)
    def _():
        to_left.start()

    share_start("bricks", infos, info, send, recv)
    infos[me] = info[...]
    find_first(foot, at)

    @pl.when(me == 0)
    def _():
        low[...] = jnp.zeros_like(low)

    @pl.when(me == n - 1)
    def _():
        high[...] = jnp.zeros_like(high)

    share_wait("bricks", infos, info, send, recv)

    @pl.when(me < n - 1)
    def _():
        to_right.wait_send()
        to_left.wait_recv()

    @pl.when(me > 0)
    def _():
        to_left.wait_send()
        to_right.wait_recv()


def flux_of(difference):
    below = 1.0 + difference * difference
    near = pl.reciprocal(below, approx=True)
    return difference * (near * (2.0 - below * near))


def sweep(load, store, planes, rows, shape):
    lane = lax.broadcasted_iota(jnp.int32, shape, 1)
    width = shape[1]

    def row(z, fluxes):
        out = []
        center = load(1, z)
        flux_x = flux_of(center - load(0, z))
        for x in range(planes):
            right = load(x + 2, z)
            next_x = flux_of(right - center)
            ahead = load(x + 1, jnp.minimum(z + 1, rows - 1))
            ahead = jnp.where(z + 1 < rows, ahead, 0.0)
            next_z = flux_of(ahead - center)
            beside = jnp.where(lane == width - 1, 0.0, pltpu.roll(center, width - 1, 1))
            next_y = flux_of(beside - center)
            edge = flux_of(center[:, :LANES])
            edge = jnp.concatenate([edge, jnp.zeros((shape[0], width - LANES), jnp.float32)], axis=1)
            prev_y = jnp.where(lane == 0, edge, pltpu.roll(next_y, 1, 1))
            total = (next_x - flux_x) + (next_z - fluxes[x]) + (next_y - prev_y)
            store(x, z, center + TIME_STEP * total)
            out.append(next_z)
            flux_x = next_x
            center = right
        return tuple(out)

    first = tuple(flux_of(load(x + 1, 0)) for x in range(planes))
    lax.fori_loop(0, rows, row, first)


def side_by_side(ref):
    return jnp.concatenate([ref[s] for s in range(ref.shape[0])], axis=1)


def unpacked(packed, frames, groups):
    count = frames // groups
    width = packed.shape[1] // groups
    cuts = [packed[:count, g * width : (g + 1) * width] for g in range(groups)]
    return jnp.concatenate(cuts, axis=0), packed[count : count + 1, :width]


def local_kernel(
    tiles, at, rec, low, high, foot, infos, columns, message, windows, own, slot_traces, one, two, y_tiles
):
    n = lax.axis_size("bricks")
    me = lax.axis_index("bricks")
    planes, rows, frames, width = rec.shape
    slots = foot.shape[0]
    shape = (frames, width)
    per = width // LANES

    def load_first(x, z):
        if x < SWEEPS:
            return low[x, z].astype(jnp.float32)
        if x < SWEEPS + planes:
            return rec[x - SWEEPS, z].astype(jnp.float32)
        return high[x - SWEEPS - planes, z].astype(jnp.float32)

    def keep(ref, margin):
        def store(x, z, value):
            if x < margin:
                value = jnp.where(me > 0, value, 0.0)
            if x >= planes + margin:
                value = jnp.where(me < n - 1, value, 0.0)
            ref[x, z] = value

        return store

    def store_last(x, z, value):
        value = value.astype(jnp.bfloat16)
        for h in range(per):
            y_tiles[(x * rows + z) * per + h] = value[:, h * LANES : (h + 1) * LANES]

    sweep(load_first, keep(one, 2), planes + 4, rows, shape)
    sweep(lambda x, z: one[x, z], keep(two, 1), planes + 2, rows, shape)
    sweep(lambda x, z: two[x, z], store_last, planes, rows, shape)

    sub = lax.broadcasted_iota(jnp.int32, (slots, 2 * LANES), 0)
    mine = jnp.zeros((slots, 2 * LANES), jnp.float32)
    for k in range(slots):
        t = at[k, 0]
        u = lax.rem(t + 1, tiles)
        rows_a = jnp.concatenate(
            [
                foot[:, pl.ds(pl.multiple_of(t * LANES, LANES), LANES)],
                foot[:, pl.ds(pl.multiple_of(u * LANES, LANES), LANES)],
            ],
            axis=1,
        )
        windows[k, frames:, :] = rows_a
        windows[k, :frames, :] = jnp.concatenate([y_tiles[t], y_tiles[u]], axis=1)
        mine = jnp.where(sub == k, rows_a.astype(jnp.float32), mine)
    own[...] = mine
    mine_bf = mine.astype(jnp.bfloat16)
    wide = frames + slots
    lane = lax.broadcasted_iota(jnp.int32, (wide, slots), 1)
    both = jnp.zeros((wide, slots), jnp.float32)
    for k in range(slots):
        found = lax.dot_general(
            windows[k], mine_bf, (((1,), (1,)), ((), ())), preferred_element_type=jnp.float32
        )
        both = jnp.where(lane == k, found, both)
    correlation = both[frames:]
    groups = LANES // slots
    count = frames // groups
    lane = lax.broadcasted_iota(jnp.int32, (LANES, n * LANES), 1)
    place = (lane // LANES * slots + lane % slots) * groups + lane % LANES // slots
    picks = jnp.where(place == columns[...], 1.0, 0.0).astype(jnp.bfloat16)
    prior = lax.dot_general(
        side_by_side(infos).astype(jnp.bfloat16),
        picks,
        (((1,), (1,)), ((), ())),
        preferred_element_type=jnp.float32,
    )
    prior, _ = unpacked(prior, frames, groups)
    slot_traces[...] = prior
    partial = both[:frames] - jnp.dot(prior, correlation, precision=HIGHEST)
    eye = lax.broadcasted_iota(jnp.int32, (slots, slots), 0) == lax.broadcasted_iota(
        jnp.int32, (slots, slots), 1
    )
    diag = jnp.sum(jnp.where(eye, correlation, 0.0), axis=0, keepdims=True)
    message[...] = jnp.zeros_like(message)
    for g in range(groups):
        message[:count, g * slots : (g + 1) * slots] = partial[g * count : (g + 1) * count]
    message[count : count + 1, :slots] = diag


def split3(value):
    a = value.astype(jnp.bfloat16)
    rest = value - a.astype(jnp.float32)
    b = rest.astype(jnp.bfloat16)
    c = (rest - b.astype(jnp.float32)).astype(jnp.bfloat16)
    return a, b, c


def second_exchange(
    frames, message, infos, wanted, prior, windows, own, new_out, result,
    gathered, same, grad, grads, send, recv, gsend, grecv,
):
    n = lax.axis_size("bricks")
    me = lax.axis_index("bricks")
    groups = lax.axis_size("frames")
    slots = own.shape[0]
    meet(("bricks", "frames"))
    share_start("bricks", gathered, message, send, recv)
    gathered[me] = message[...]
    count = frames // (LANES // slots)
    for s in range(n):
        row = infos[s][count : count + 1, :]
        same[:, s * LANES : (s + 1) * LANES] = jnp.where(wanted[...] == row, 1.0, 0.0).astype(
            jnp.bfloat16
        )
    share_wait("bricks", gathered, message, send, recv)
    parts = [part.astype(jnp.float32) for part in split3(side_by_side(gathered))]
    parts = jnp.concatenate(parts, axis=0).astype(jnp.bfloat16)
    found = lax.dot_general(
        parts, same[...], (((1,), (1,)), ((), ())), preferred_element_type=jnp.float32
    )
    high = message.shape[0]
    found = found[:high] + found[high : 2 * high] + found[2 * high :]
    summed, diag = unpacked(found, frames, LANES // slots)
    new = jnp.maximum(0.0, prior[...] + summed / (diag + 1.0))
    new_out[...] = new[:, slots:]
    turn = lax.broadcasted_iota(jnp.int32, (slots, slots), 0) == lax.broadcasted_iota(
        jnp.int32, (slots, slots), 1
    )
    picked = lax.dot_general(
        jnp.where(turn, 1.0, 0.0).astype(jnp.bfloat16),
        new[:, :slots].astype(jnp.bfloat16),
        (((1,), (1,)), ((), ())),
        preferred_element_type=jnp.float32,
    ).astype(jnp.bfloat16)
    gram = lax.dot_general(
        picked, picked, (((1,), (1,)), ((), ())), preferred_element_type=jnp.float32
    )
    g1, g2, g3 = split3(gram)
    none = jnp.zeros((slots, frames), jnp.float32)
    left = jnp.concatenate(
        [
            jnp.concatenate([picked.astype(jnp.float32), -g1.astype(jnp.float32)], axis=1),
            jnp.concatenate([none, -g2.astype(jnp.float32)], axis=1),
            jnp.concatenate([none, -g3.astype(jnp.float32)], axis=1),
        ],
        axis=0,
    ).astype(jnp.bfloat16)
    sub = lax.broadcasted_iota(jnp.int32, (slots, 2 * LANES), 0)
    total = jnp.zeros((slots, 2 * LANES), jnp.float32)
    for k in range(slots):
        one = jnp.dot(left, windows[k], preferred_element_type=jnp.float32)
        one = one[:slots] + one[slots : 2 * slots] + one[2 * slots :]
        total = jnp.where(sub == k, one, total)
    eye = lax.broadcasted_iota(jnp.int32, (slots, slots), 0) == lax.broadcasted_iota(
        jnp.int32, (slots, slots), 1
    )
    gdiag = jnp.sum(jnp.where(eye, gram, 0.0), axis=1, keepdims=True)
    grad[:, : 2 * LANES] = total
    grad[:, 2 * LANES :] = jnp.broadcast_to(gdiag, (slots, LANES))
    share_start("frames", grads, grad, gsend, grecv)
    grads[lax.axis_index("frames")] = grad[...]
    share_wait("frames", grads, grad, gsend, grecv)
    whole = grads[0]
    for g in range(1, groups):
        whole = whole + grads[g]
    current = own[...]
    step = whole[:, : 2 * LANES] / (whole[:, 2 * LANES : 2 * LANES + 1] + 1.0)
    result[...] = jnp.where(current > 0, jnp.maximum(current + step, 0.0), 0.0)


def spread_kernel(tiles, at, result, new, out, new_out):
    slots, width = out.shape
    base = pl.program_id(0) * (width // LANES)
    first = at[...] - base
    second = jnp.where(at[...] + 1 == tiles, 0, at[...] + 1) - base
    head = result[:, :LANES]
    tail = result[:, LANES:]
    for t in range(width // LANES):
        out[:, t * LANES : (t + 1) * LANES] = jnp.where(
            first == t, head, jnp.where(second == t, tail, 0.0)
        ).astype(jnp.bfloat16)
    new_out[...] = new[...]


def shards(recording, traces, footprints, block_owner, block_slot):
    frames, planes, rows, width = recording.shape
    slots, voxels = footprints.shape
    owned = traces.shape[1]
    n = lax.axis_size("bricks")
    groups = lax.axis_size("frames")
    me = lax.axis_index("bricks")
    tiles = voxels // LANES
    f32 = jnp.float32
    sds = jax.ShapeDtypeStruct
    dma = pltpu.SemaphoreType.DMA
    component = block_owner[:, 0] * owned + block_slot
    rec = jnp.transpose(recording, (1, 2, 0, 3))
    packs = LANES // slots
    count = frames // packs
    high_rows = -(-(count + 1) // 8) * 8
    info = traces.astype(f32).reshape(packs, count, owned).transpose(1, 0, 2).reshape(count, LANES)
    extra = component[None, :] * packs + jnp.arange(packs, dtype=jnp.int32)[:, None]
    extra = jnp.pad(extra.astype(f32).reshape(1, LANES), ((0, high_rows - count - 1), (0, 0)))
    info = jnp.concatenate([info, extra], axis=0)
    order = jnp.arange(packs, dtype=jnp.int32)[:, None]
    columns = (component[None, :] * packs + order).reshape(packs * slots, 1)
    mine = me * owned + jnp.arange(owned, dtype=jnp.int32)
    both = jnp.concatenate([component, mine])
    wanted = (both[None, :] * packs + order).reshape(packs * (slots + owned), 1).astype(f32)

    low, high, infos, at = pl.pallas_call(
        first_exchange,
        out_shape=(
            sds((SWEEPS, rows, frames, width), jnp.bfloat16),
            sds((SWEEPS, rows, frames, width), jnp.bfloat16),
            sds((n,) + info.shape, f32),
            sds((slots, LANES), jnp.int32),
        ),
        in_specs=[VMEM] * 3,
        out_specs=(VMEM,) * 4,
        scratch_shapes=[dma((2,)), dma((2,)), dma((n,)), dma((n,))],
        compiler_params=pltpu.CompilerParams(
            collective_id=0, has_side_effects=True, vmem_limit_bytes=16 << 20
        ),
        name="first_exchange",
    )(rec, info, footprints)

    message, windows, own, slot_traces = pl.pallas_call(
        functools.partial(local_kernel, tiles),
        out_shape=(
            sds((high_rows, LANES), f32),
            sds((slots, frames + slots, 2 * LANES), jnp.bfloat16),
            sds((slots, 2 * LANES), f32),
            sds((frames, slots), f32),
        ),
        in_specs=[SMEM] + [VMEM] * 6,
        out_specs=(VMEM,) * 4,
        scratch_shapes=[
            pltpu.VMEM((planes + 4, rows, frames, width), f32),
            pltpu.VMEM((planes + 2, rows, frames, width), f32),
            pltpu.VMEM((tiles, frames, LANES), jnp.bfloat16),
        ],
        compiler_params=pltpu.CompilerParams(vmem_limit_bytes=32 << 20),
        name="denoise_project",
    )(at, rec, low, high, footprints, infos, columns)

    prior = jnp.concatenate([slot_traces, traces.astype(f32)], axis=1)

    new, result = pl.pallas_call(
        functools.partial(second_exchange, frames),
        out_shape=(sds((frames, owned), f32), sds((slots, 2 * LANES), f32)),
        in_specs=[VMEM] * 6,
        out_specs=(VMEM, VMEM),
        scratch_shapes=[
            pltpu.VMEM((n, high_rows, LANES), f32),
            pltpu.VMEM((packs * (slots + owned), n * LANES), jnp.bfloat16),
            pltpu.VMEM((slots, 3 * LANES), f32),
            pltpu.VMEM((groups, slots, 3 * LANES), f32),
            dma((n,)),
            dma((n,)),
            dma((groups,)),
            dma((groups,)),
        ],
        compiler_params=pltpu.CompilerParams(
            collective_id=1, has_side_effects=True, vmem_limit_bytes=16 << 20
        ),
        name="second_exchange",
    )(message, infos, wanted, prior, windows, own)

    steps = 4 if tiles % 4 == 0 else 1
    footprints_new, traces_new = pl.pallas_call(
        functools.partial(spread_kernel, tiles),
        out_shape=(sds((slots, voxels), jnp.bfloat16), sds((frames, owned), f32)),
        grid=(steps,),
        in_specs=[
            pl.BlockSpec((slots, LANES), lambda i: (0, 0)),
            pl.BlockSpec((slots, 2 * LANES), lambda i: (0, 0)),
            pl.BlockSpec((frames, owned), lambda i: (0, 0)),
        ],
        out_specs=(
            pl.BlockSpec((slots, voxels // steps), lambda i: (0, i)),
            pl.BlockSpec((frames, owned), lambda i: (0, 0)),
        ),
        name="spread",
    )(at, result, new)
    return (traces_new, footprints_new)


def solution(mesh):
    return jax.shard_map(
        shards,
        mesh=mesh,
        in_specs=(
            P("frames", "bricks", None, None),
            P("frames", "bricks"),
            P("bricks", None),
            P("bricks", None),
            P("bricks"),
        ),
        out_specs=(P("frames", "bricks"), P("bricks", None)),
        check_vma=False,
    )
```

```python
import functools

import jax
import jax.numpy as jnp
from jax import lax
from jax.experimental import pallas as pl
from jax.experimental.pallas import tpu as pltpu
from jax.sharding import PartitionSpec as P

TIME_STEP = 0.14
SWEEPS = 3
CUTS = 4
LANES = 128
HIGHEST = lax.Precision.HIGHEST
MESH = pl.DeviceIdType.MESH
VMEM = pl.BlockSpec(memory_space=pltpu.VMEM)
SMEM = pl.BlockSpec(memory_space=pltpu.SMEM)


def meet(axes):
    barrier = pltpu.get_barrier_semaphore()
    total = 0
    for axis in axes:
        count = lax.axis_size(axis)
        me = lax.axis_index(axis)

        def tell(d, carry, axis=axis, count=count, me=me):
            pl.semaphore_signal(
                barrier, inc=1, device_id={axis: lax.rem(me + d, count)}, device_id_type=MESH
            )
            return carry

        lax.fori_loop(1, count, tell, 0)
        total += count - 1
    pl.semaphore_wait(barrier, total)


def share_copy(axis, gathered, source, send, recv, d):
    count = lax.axis_size(axis)
    me = lax.axis_index(axis)
    return pltpu.make_async_remote_copy(
        src_ref=source,
        dst_ref=gathered.at[me],
        send_sem=send.at[d],
        recv_sem=recv.at[d],
        device_id={axis: lax.rem(me + d, count)},
        device_id_type=MESH,
    )


def share_start(axis, gathered, source, send, recv):
    def go(d, carry):
        share_copy(axis, gathered, source, send, recv, d).start()
        return carry

    lax.fori_loop(1, lax.axis_size(axis), go, 0)


def share_wait(axis, gathered, source, send, recv):
    def go(d, carry):
        share_copy(axis, gathered, source, send, recv, d).wait()
        return carry

    lax.fori_loop(1, lax.axis_size(axis), go, 0)


def find_first(foot, at):
    tiles = foot.shape[1] // LANES
    where = jnp.zeros((foot.shape[0], LANES), jnp.int32)
    for t in range(tiles):
        cut = foot[:, t * LANES : (t + 1) * LANES].astype(jnp.float32)
        where = jnp.where(cut > 0, t, where)
    at[...] = jnp.broadcast_to(where[:, LANES - 1 :], where.shape)


def flux_of(difference):
    below = 1.0 + difference * difference
    near = pl.reciprocal(below, approx=True)
    return difference * (near * (2.0 - below * near))


def sweep(load, store, planes, rows, shape, low_row, high_row, first):
    lane = lax.broadcasted_iota(jnp.int32, shape, 1)
    width = shape[1]

    def row(z, fluxes):
        out = []
        center = load(1, z)
        flux_x = flux_of(center - load(0, z))
        for x in range(planes):
            right = load(x + 2, z)
            next_x = flux_of(right - center)
            ahead = load(x + 1, jnp.minimum(z + 1, rows - 1))
            ahead = jnp.where(z + 1 < rows, ahead, 0.0)
            next_z = flux_of(ahead - center)
            beside = jnp.where(lane == width - 1, 0.0, pltpu.roll(center, width - 1, 1))
            next_y = flux_of(beside - center)
            edge = flux_of(center[:, :LANES])
            edge = jnp.concatenate([edge, jnp.zeros((shape[0], width - LANES), jnp.float32)], axis=1)
            prev_y = jnp.where(lane == 0, edge, pltpu.roll(next_y, 1, 1))
            total = (next_x - flux_x) + (next_z - fluxes[x]) + (next_y - prev_y)
            store(x, z, center + TIME_STEP * total)
            out.append(next_z)
            flux_x = next_x
            center = right
        return tuple(out)

    if first is None:
        first = tuple(flux_of(load(x + 1, 0)) for x in range(planes))
    return lax.fori_loop(low_row, high_row, row, first)


def first_exchange(
    rec, info, foot, y_tiles, infos, at, low, high, one, two, hsend, hrecv, send, recv
):
    n = lax.axis_size("bricks")
    me = lax.axis_index("bricks")
    planes, rows, frames, width = rec.shape
    shape = (frames, width)
    per = width // LANES
    cuts = CUTS if rows % CUTS == 0 and rows // CUTS > SWEEPS else 1
    part = rows // cuts
    meet(("bricks",))

    def copies(c):
        at_rows = pl.ds(c * part, part)
        to_right = pltpu.make_async_remote_copy(
            src_ref=rec.at[pl.ds(planes - SWEEPS, SWEEPS), at_rows],
            dst_ref=low.at[:, at_rows],
            send_sem=hsend.at[0, c],
            recv_sem=hrecv.at[0, c],
            device_id={"bricks": lax.rem(me + 1, n)},
            device_id_type=MESH,
        )
        to_left = pltpu.make_async_remote_copy(
            src_ref=rec.at[pl.ds(0, SWEEPS), at_rows],
            dst_ref=high.at[:, at_rows],
            send_sem=hsend.at[1, c],
            recv_sem=hrecv.at[1, c],
            device_id={"bricks": lax.rem(me + n - 1, n)},
            device_id_type=MESH,
        )
        return to_right, to_left

    for c in range(cuts):
        to_right, to_left = copies(c)
        pl.when(me < n - 1)(to_right.start)
        pl.when(me > 0)(to_left.start)
    share_start("bricks", infos, info, send, recv)
    infos[me] = info[...]

    @pl.when(me == 0)
    def _():
        low[...] = jnp.zeros_like(low)

    @pl.when(me == n - 1)
    def _():
        high[...] = jnp.zeros_like(high)

    find_first(foot, at)

    def load_first(x, z):
        if x < SWEEPS:
            return low[x, z].astype(jnp.float32)
        if x < SWEEPS + planes:
            return rec[x - SWEEPS, z].astype(jnp.float32)
        return high[x - SWEEPS - planes, z].astype(jnp.float32)

    def keep(ref, margin):
        def store(x, z, value):
            if x < margin:
                value = jnp.where(me > 0, value, 0.0)
            if x >= planes + margin:
                value = jnp.where(me < n - 1, value, 0.0)
            ref[x, z] = value

        return store

    def store_last(x, z, value):
        value = value.astype(jnp.bfloat16)
        for h in range(per):
            y_tiles[(x * rows + z) * per + h] = value[:, h * LANES : (h + 1) * LANES]

    loads = (load_first, lambda x, z: one[x, z], lambda x, z: two[x, z])
    stores = (keep(one, 2), keep(two, 1), store_last)
    carried = [None] * SWEEPS
    done = [0] * SWEEPS
    for c in range(cuts):
        to_right, to_left = copies(c)
        pl.when(me > 0)(to_right.wait_recv)
        pl.when(me < n - 1)(to_left.wait_recv)
        for i in range(SWEEPS):
            end = rows if c == cuts - 1 else (c + 1) * part - 1 - i
            carried[i] = sweep(
                loads[i], stores[i], planes + 2 * (SWEEPS - 1 - i), rows, shape, done[i], end, carried[i]
            )
            done[i] = end
    for c in range(cuts):
        to_right, to_left = copies(c)
        pl.when(me < n - 1)(to_right.wait_send)
        pl.when(me > 0)(to_left.wait_send)
    share_wait("bricks", infos, info, send, recv)


def side_by_side(ref):
    return jnp.concatenate([ref[s] for s in range(ref.shape[0])], axis=1)


def unpacked(packed, frames, groups):
    count = frames // groups
    width = packed.shape[1] // groups
    cuts = [packed[:count, g * width : (g + 1) * width] for g in range(groups)]
    return jnp.concatenate(cuts, axis=0), packed[count : count + 1, :width]


def local_kernel(
    tiles, at, y_tiles, foot, infos, columns, message, windows, own, slot_traces
):
    n = lax.axis_size("bricks")
    slots = foot.shape[0]
    frames = y_tiles.shape[1]
    sub = lax.broadcasted_iota(jnp.int32, (slots, 2 * LANES), 0)
    mine = jnp.zeros((slots, 2 * LANES), jnp.float32)
    for k in range(slots):
        t = at[k, 0]
        u = lax.rem(t + 1, tiles)
        rows_a = jnp.concatenate(
            [
                foot[:, pl.ds(pl.multiple_of(t * LANES, LANES), LANES)],
                foot[:, pl.ds(pl.multiple_of(u * LANES, LANES), LANES)],
            ],
            axis=1,
        )
        windows[k, frames:, :] = rows_a
        windows[k, :frames, :] = jnp.concatenate([y_tiles[t], y_tiles[u]], axis=1)
        mine = jnp.where(sub == k, rows_a.astype(jnp.float32), mine)
    own[...] = mine
    mine_bf = mine.astype(jnp.bfloat16)
    wide = frames + slots
    lane = lax.broadcasted_iota(jnp.int32, (wide, slots), 1)
    both = jnp.zeros((wide, slots), jnp.float32)
    for k in range(slots):
        found = lax.dot_general(
            windows[k], mine_bf, (((1,), (1,)), ((), ())), preferred_element_type=jnp.float32
        )
        both = jnp.where(lane == k, found, both)
    correlation = both[frames:]
    groups = LANES // slots
    count = frames // groups
    lane = lax.broadcasted_iota(jnp.int32, (LANES, n * LANES), 1)
    place = (lane // LANES * slots + lane % slots) * groups + lane % LANES // slots
    picks = jnp.where(place == columns[...], 1.0, 0.0).astype(jnp.bfloat16)
    prior = lax.dot_general(
        side_by_side(infos).astype(jnp.bfloat16),
        picks,
        (((1,), (1,)), ((), ())),
        preferred_element_type=jnp.float32,
    )
    prior, _ = unpacked(prior, frames, groups)
    slot_traces[...] = prior
    partial = both[:frames] - jnp.dot(prior, correlation, precision=HIGHEST)
    eye = lax.broadcasted_iota(jnp.int32, (slots, slots), 0) == lax.broadcasted_iota(
        jnp.int32, (slots, slots), 1
    )
    diag = jnp.sum(jnp.where(eye, correlation, 0.0), axis=0, keepdims=True)
    message[...] = jnp.zeros_like(message)
    for g in range(groups):
        message[:count, g * slots : (g + 1) * slots] = partial[g * count : (g + 1) * count]
    message[count : count + 1, :slots] = diag


def split3(value):
    a = value.astype(jnp.bfloat16)
    rest = value - a.astype(jnp.float32)
    b = rest.astype(jnp.bfloat16)
    c = (rest - b.astype(jnp.float32)).astype(jnp.bfloat16)
    return a, b, c


def second_exchange(
    frames, message, infos, wanted, prior, windows, own, new_out, result,
    gathered, same, grad, grads, send, recv, gsend, grecv,
):
    n = lax.axis_size("bricks")
    me = lax.axis_index("bricks")
    groups = lax.axis_size("frames")
    slots = own.shape[0]
    meet(("bricks", "frames"))
    share_start("bricks", gathered, message, send, recv)
    gathered[me] = message[...]
    count = frames // (LANES // slots)
    for s in range(n):
        row = infos[s][count : count + 1, :]
        same[:, s * LANES : (s + 1) * LANES] = jnp.where(wanted[...] == row, 1.0, 0.0).astype(
            jnp.bfloat16
        )
    share_wait("bricks", gathered, message, send, recv)
    parts = [part.astype(jnp.float32) for part in split3(side_by_side(gathered))]
    parts = jnp.concatenate(parts, axis=0).astype(jnp.bfloat16)
    found = lax.dot_general(
        parts, same[...], (((1,), (1,)), ((), ())), preferred_element_type=jnp.float32
    )
    high = message.shape[0]
    found = found[:high] + found[high : 2 * high] + found[2 * high :]
    summed, diag = unpacked(found, frames, LANES // slots)
    new = jnp.maximum(0.0, prior[...] + summed / (diag + 1.0))
    new_out[...] = new[:, slots:]
    turn = lax.broadcasted_iota(jnp.int32, (slots, slots), 0) == lax.broadcasted_iota(
        jnp.int32, (slots, slots), 1
    )
    picked = lax.dot_general(
        jnp.where(turn, 1.0, 0.0).astype(jnp.bfloat16),
        new[:, :slots].astype(jnp.bfloat16),
        (((1,), (1,)), ((), ())),
        preferred_element_type=jnp.float32,
    ).astype(jnp.bfloat16)
    gram = lax.dot_general(
        picked, picked, (((1,), (1,)), ((), ())), preferred_element_type=jnp.float32
    )
    g1, g2, g3 = split3(gram)
    none = jnp.zeros((slots, frames), jnp.float32)
    left = jnp.concatenate(
        [
            jnp.concatenate([picked.astype(jnp.float32), -g1.astype(jnp.float32)], axis=1),
            jnp.concatenate([none, -g2.astype(jnp.float32)], axis=1),
            jnp.concatenate([none, -g3.astype(jnp.float32)], axis=1),
        ],
        axis=0,
    ).astype(jnp.bfloat16)
    sub = lax.broadcasted_iota(jnp.int32, (slots, 2 * LANES), 0)
    total = jnp.zeros((slots, 2 * LANES), jnp.float32)
    for k in range(slots):
        one = jnp.dot(left, windows[k], preferred_element_type=jnp.float32)
        one = one[:slots] + one[slots : 2 * slots] + one[2 * slots :]
        total = jnp.where(sub == k, one, total)
    eye = lax.broadcasted_iota(jnp.int32, (slots, slots), 0) == lax.broadcasted_iota(
        jnp.int32, (slots, slots), 1
    )
    gdiag = jnp.sum(jnp.where(eye, gram, 0.0), axis=1, keepdims=True)
    grad[:, : 2 * LANES] = total
    grad[:, 2 * LANES :] = jnp.broadcast_to(gdiag, (slots, LANES))
    share_start("frames", grads, grad, gsend, grecv)
    grads[lax.axis_index("frames")] = grad[...]
    share_wait("frames", grads, grad, gsend, grecv)
    whole = grads[0]
    for g in range(1, groups):
        whole = whole + grads[g]
    current = own[...]
    step = whole[:, : 2 * LANES] / (whole[:, 2 * LANES : 2 * LANES + 1] + 1.0)
    result[...] = jnp.where(current > 0, jnp.maximum(current + step, 0.0), 0.0)


def spread_kernel(tiles, at, result, new, out, new_out):
    slots, width = out.shape
    base = pl.program_id(0) * (width // LANES)
    first = at[...] - base
    second = jnp.where(at[...] + 1 == tiles, 0, at[...] + 1) - base
    head = result[:, :LANES]
    tail = result[:, LANES:]
    for t in range(width // LANES):
        out[:, t * LANES : (t + 1) * LANES] = jnp.where(
            first == t, head, jnp.where(second == t, tail, 0.0)
        ).astype(jnp.bfloat16)
    new_out[...] = new[...]


def shards(recording, traces, footprints, block_owner, block_slot):
    frames, planes, rows, width = recording.shape
    slots, voxels = footprints.shape
    owned = traces.shape[1]
    n = lax.axis_size("bricks")
    groups = lax.axis_size("frames")
    me = lax.axis_index("bricks")
    tiles = voxels // LANES
    f32 = jnp.float32
    sds = jax.ShapeDtypeStruct
    dma = pltpu.SemaphoreType.DMA
    component = block_owner[:, 0] * owned + block_slot
    rec = jnp.transpose(recording, (1, 2, 0, 3))
    packs = LANES // slots
    count = frames // packs
    high_rows = -(-(count + 1) // 8) * 8
    info = traces.astype(f32).reshape(packs, count, owned).transpose(1, 0, 2).reshape(count, LANES)
    extra = component[None, :] * packs + jnp.arange(packs, dtype=jnp.int32)[:, None]
    extra = jnp.pad(extra.astype(f32).reshape(1, LANES), ((0, high_rows - count - 1), (0, 0)))
    info = jnp.concatenate([info, extra], axis=0)
    order = jnp.arange(packs, dtype=jnp.int32)[:, None]
    columns = (component[None, :] * packs + order).reshape(packs * slots, 1)
    mine = me * owned + jnp.arange(owned, dtype=jnp.int32)
    both = jnp.concatenate([component, mine])
    wanted = (both[None, :] * packs + order).reshape(packs * (slots + owned), 1).astype(f32)

    y_tiles, infos, at = pl.pallas_call(
        first_exchange,
        out_shape=(
            sds((tiles, frames, LANES), jnp.bfloat16),
            sds((n,) + info.shape, f32),
            sds((slots, LANES), jnp.int32),
        ),
        in_specs=[VMEM] * 3,
        out_specs=(VMEM,) * 3,
        scratch_shapes=[
            pltpu.VMEM((SWEEPS, rows, frames, width), jnp.bfloat16),
            pltpu.VMEM((SWEEPS, rows, frames, width), jnp.bfloat16),
            pltpu.VMEM((planes + 4, rows, frames, width), f32),
            pltpu.VMEM((planes + 2, rows, frames, width), f32),
            dma((2, CUTS)),
            dma((2, CUTS)),
            dma((n,)),
            dma((n,)),
        ],
        compiler_params=pltpu.CompilerParams(
            collective_id=0, has_side_effects=True, vmem_limit_bytes=32 << 20
        ),
        name="first_exchange",
    )(rec, info, footprints)

    message, windows, own, slot_traces = pl.pallas_call(
        functools.partial(local_kernel, tiles),
        out_shape=(
            sds((high_rows, LANES), f32),
            sds((slots, frames + slots, 2 * LANES), jnp.bfloat16),
            sds((slots, 2 * LANES), f32),
            sds((frames, slots), f32),
        ),
        in_specs=[SMEM] + [VMEM] * 4,
        out_specs=(VMEM,) * 4,
        compiler_params=pltpu.CompilerParams(vmem_limit_bytes=32 << 20),
        name="project",
    )(at, y_tiles, footprints, infos, columns)

    prior = jnp.concatenate([slot_traces, traces.astype(f32)], axis=1)

    new, result = pl.pallas_call(
        functools.partial(second_exchange, frames),
        out_shape=(sds((frames, owned), f32), sds((slots, 2 * LANES), f32)),
        in_specs=[VMEM] * 6,
        out_specs=(VMEM, VMEM),
        scratch_shapes=[
            pltpu.VMEM((n, high_rows, LANES), f32),
            pltpu.VMEM((packs * (slots + owned), n * LANES), jnp.bfloat16),
            pltpu.VMEM((slots, 3 * LANES), f32),
            pltpu.VMEM((groups, slots, 3 * LANES), f32),
            dma((n,)),
            dma((n,)),
            dma((groups,)),
            dma((groups,)),
        ],
        compiler_params=pltpu.CompilerParams(
            collective_id=1, has_side_effects=True, vmem_limit_bytes=16 << 20
        ),
        name="second_exchange",
    )(message, infos, wanted, prior, windows, own)

    steps = 4 if tiles % 4 == 0 else 1
    footprints_new, traces_new = pl.pallas_call(
        functools.partial(spread_kernel, tiles),
        out_shape=(sds((slots, voxels), jnp.bfloat16), sds((frames, owned), f32)),
        grid=(steps,),
        in_specs=[
            pl.BlockSpec((slots, LANES), lambda i: (0, 0)),
            pl.BlockSpec((slots, 2 * LANES), lambda i: (0, 0)),
            pl.BlockSpec((frames, owned), lambda i: (0, 0)),
        ],
        out_specs=(
            pl.BlockSpec((slots, voxels // steps), lambda i: (0, i)),
            pl.BlockSpec((frames, owned), lambda i: (0, 0)),
        ),
        name="spread",
    )(at, result, new)
    return (traces_new, footprints_new)


def solution(mesh):
    return jax.shard_map(
        shards,
        mesh=mesh,
        in_specs=(
            P("frames", "bricks", None, None),
            P("frames", "bricks"),
            P("bricks", None),
            P("bricks", None),
            P("bricks"),
        ),
        out_specs=(P("frames", "bricks"), P("bricks", None)),
        check_vma=False,
    )
```

```python
import functools

import jax
import jax.numpy as jnp
from jax import lax
from jax.experimental import pallas as pl
from jax.experimental.pallas import tpu as pltpu
from jax.sharding import PartitionSpec as P

TIME_STEP = 0.14
SWEEPS = 3
CUTS = 8
LANES = 128
HIGHEST = lax.Precision.HIGHEST
MESH = pl.DeviceIdType.MESH
VMEM = pl.BlockSpec(memory_space=pltpu.VMEM)
SMEM = pl.BlockSpec(memory_space=pltpu.SMEM)


def meet(axes):
    barrier = pltpu.get_barrier_semaphore()
    total = 0
    for axis in axes:
        count = lax.axis_size(axis)
        me = lax.axis_index(axis)

        def tell(d, carry, axis=axis, count=count, me=me):
            pl.semaphore_signal(
                barrier, inc=1, device_id={axis: lax.rem(me + d, count)}, device_id_type=MESH
            )
            return carry

        lax.fori_loop(1, count, tell, 0)
        total += count - 1
    pl.semaphore_wait(barrier, total)


def share_copy(axis, gathered, source, send, recv, d):
    count = lax.axis_size(axis)
    me = lax.axis_index(axis)
    return pltpu.make_async_remote_copy(
        src_ref=source,
        dst_ref=gathered.at[me],
        send_sem=send.at[d],
        recv_sem=recv.at[d],
        device_id={axis: lax.rem(me + d, count)},
        device_id_type=MESH,
    )


def share_start(axis, gathered, source, send, recv):
    def go(d, carry):
        share_copy(axis, gathered, source, send, recv, d).start()
        return carry

    lax.fori_loop(1, lax.axis_size(axis), go, 0)


def share_wait(axis, gathered, source, send, recv):
    def go(d, carry):
        share_copy(axis, gathered, source, send, recv, d).wait()
        return carry

    lax.fori_loop(1, lax.axis_size(axis), go, 0)


def find_first(foot, at):
    tiles = foot.shape[1] // LANES
    where = jnp.zeros((foot.shape[0], LANES), jnp.int32)
    for t in range(tiles):
        cut = foot[:, t * LANES : (t + 1) * LANES].astype(jnp.float32)
        where = jnp.where(cut > 0, t, where)
    at[...] = jnp.broadcast_to(where[:, LANES - 1 :], where.shape)


def flux_of(difference):
    below = 1.0 + difference * difference
    near = pl.reciprocal(below, approx=True)
    return difference * (near * (2.0 - below * near))


def sweep(load, store, planes, rows, shape, low_row, high_row, first):
    lane = lax.broadcasted_iota(jnp.int32, shape, 1)
    width = shape[1]

    def row(z, fluxes):
        out = []
        center = load(1, z)
        flux_x = flux_of(center - load(0, z))
        for x in range(planes):
            right = load(x + 2, z)
            next_x = flux_of(right - center)
            ahead = load(x + 1, jnp.minimum(z + 1, rows - 1))
            ahead = jnp.where(z + 1 < rows, ahead, 0.0)
            next_z = flux_of(ahead - center)
            beside = jnp.where(lane == width - 1, 0.0, pltpu.roll(center, width - 1, 1))
            next_y = flux_of(beside - center)
            edge = flux_of(center[:, :LANES])
            edge = jnp.concatenate([edge, jnp.zeros((shape[0], width - LANES), jnp.float32)], axis=1)
            prev_y = jnp.where(lane == 0, edge, pltpu.roll(next_y, 1, 1))
            total = (next_x - flux_x) + (next_z - fluxes[x]) + (next_y - prev_y)
            store(x, z, center + TIME_STEP * total)
            out.append(next_z)
            flux_x = next_x
            center = right
        return tuple(out)

    if first is None:
        first = tuple(flux_of(load(x + 1, 0)) for x in range(planes))
    return lax.fori_loop(low_row, high_row, row, first)


def first_exchange(
    rec, info, foot, y_tiles, infos, at, low, high, one, two, hsend, hrecv, send, recv
):
    n = lax.axis_size("bricks")
    me = lax.axis_index("bricks")
    planes, rows, frames, width = rec.shape
    shape = (frames, width)
    per = width // LANES
    cuts = CUTS if rows % CUTS == 0 else 1
    part = rows // cuts
    meet(("bricks",))

    def copies(c):
        at_rows = pl.ds(c * part, part)
        to_right = pltpu.make_async_remote_copy(
            src_ref=rec.at[pl.ds(planes - SWEEPS, SWEEPS), at_rows],
            dst_ref=low.at[:, at_rows],
            send_sem=hsend.at[0, c],
            recv_sem=hrecv.at[0, c],
            device_id={"bricks": lax.rem(me + 1, n)},
            device_id_type=MESH,
        )
        to_left = pltpu.make_async_remote_copy(
            src_ref=rec.at[pl.ds(0, SWEEPS), at_rows],
            dst_ref=high.at[:, at_rows],
            send_sem=hsend.at[1, c],
            recv_sem=hrecv.at[1, c],
            device_id={"bricks": lax.rem(me + n - 1, n)},
            device_id_type=MESH,
        )
        return to_right, to_left

    for c in range(cuts):
        to_right, to_left = copies(c)
        pl.when(me < n - 1)(to_right.start)
        pl.when(me > 0)(to_left.start)
    share_start("bricks", infos, info, send, recv)
    infos[me] = info[...]

    @pl.when(me == 0)
    def _():
        low[...] = jnp.zeros_like(low)

    @pl.when(me == n - 1)
    def _():
        high[...] = jnp.zeros_like(high)

    find_first(foot, at)

    def load_first(x, z):
        if x < SWEEPS:
            return low[x, z].astype(jnp.float32)
        if x < SWEEPS + planes:
            return rec[x - SWEEPS, z].astype(jnp.float32)
        return high[x - SWEEPS - planes, z].astype(jnp.float32)

    def keep(ref, margin):
        def store(x, z, value):
            if x < margin:
                value = jnp.where(me > 0, value, 0.0)
            if x >= planes + margin:
                value = jnp.where(me < n - 1, value, 0.0)
            ref[x, z] = value

        return store

    def store_last(x, z, value):
        value = value.astype(jnp.bfloat16)
        for h in range(per):
            y_tiles[(x * rows + z) * per + h] = value[:, h * LANES : (h + 1) * LANES]

    loads = (load_first, lambda x, z: one[x, z], lambda x, z: two[x, z])
    stores = (keep(one, 2), keep(two, 1), store_last)
    carried = [None] * SWEEPS
    done = [0] * SWEEPS
    for c in range(cuts):
        to_right, to_left = copies(c)
        pl.when(me > 0)(to_right.wait_recv)
        pl.when(me < n - 1)(to_left.wait_recv)
        for i in range(SWEEPS):
            end = rows if c == cuts - 1 else (c + 1) * part - 1 - i
            if end <= done[i]:
                continue
            carried[i] = sweep(
                loads[i], stores[i], planes + 2 * (SWEEPS - 1 - i), rows, shape, done[i], end, carried[i]
            )
            done[i] = end
    for c in range(cuts):
        to_right, to_left = copies(c)
        pl.when(me < n - 1)(to_right.wait_send)
        pl.when(me > 0)(to_left.wait_send)
    share_wait("bricks", infos, info, send, recv)


def side_by_side(ref):
    return jnp.concatenate([ref[s] for s in range(ref.shape[0])], axis=1)


def unpacked(packed, frames, groups):
    count = frames // groups
    width = packed.shape[1] // groups
    cuts = [packed[:count, g * width : (g + 1) * width] for g in range(groups)]
    return jnp.concatenate(cuts, axis=0), packed[count : count + 1, :width]


def local_kernel(
    tiles, at, y_tiles, foot, infos, columns, message, windows, own, slot_traces
):
    n = lax.axis_size("bricks")
    slots = foot.shape[0]
    frames = y_tiles.shape[1]
    sub = lax.broadcasted_iota(jnp.int32, (slots, 2 * LANES), 0)
    mine = jnp.zeros((slots, 2 * LANES), jnp.float32)
    for k in range(slots):
        t = at[k, 0]
        u = lax.rem(t + 1, tiles)
        rows_a = jnp.concatenate(
            [
                foot[:, pl.ds(pl.multiple_of(t * LANES, LANES), LANES)],
                foot[:, pl.ds(pl.multiple_of(u * LANES, LANES), LANES)],
            ],
            axis=1,
        )
        windows[k, frames:, :] = rows_a
        windows[k, :frames, :] = jnp.concatenate([y_tiles[t], y_tiles[u]], axis=1)
        mine = jnp.where(sub == k, rows_a.astype(jnp.float32), mine)
    own[...] = mine
    mine_bf = mine.astype(jnp.bfloat16)
    wide = frames + slots
    lane = lax.broadcasted_iota(jnp.int32, (wide, slots), 1)
    both = jnp.zeros((wide, slots), jnp.float32)
    for k in range(slots):
        found = lax.dot_general(
            windows[k], mine_bf, (((1,), (1,)), ((), ())), preferred_element_type=jnp.float32
        )
        both = jnp.where(lane == k, found, both)
    correlation = both[frames:]
    groups = LANES // slots
    count = frames // groups
    lane = lax.broadcasted_iota(jnp.int32, (LANES, n * LANES), 1)
    place = (lane // LANES * slots + lane % slots) * groups + lane % LANES // slots
    picks = jnp.where(place == columns[...], 1.0, 0.0).astype(jnp.bfloat16)
    prior = lax.dot_general(
        side_by_side(infos).astype(jnp.bfloat16),
        picks,
        (((1,), (1,)), ((), ())),
        preferred_element_type=jnp.float32,
    )
    prior, _ = unpacked(prior, frames, groups)
    slot_traces[...] = prior
    partial = both[:frames] - jnp.dot(prior, correlation, precision=HIGHEST)
    eye = lax.broadcasted_iota(jnp.int32, (slots, slots), 0) == lax.broadcasted_iota(
        jnp.int32, (slots, slots), 1
    )
    diag = jnp.sum(jnp.where(eye, correlation, 0.0), axis=0, keepdims=True)
    message[...] = jnp.zeros_like(message)
    for g in range(groups):
        message[:count, g * slots : (g + 1) * slots] = partial[g * count : (g + 1) * count]
    message[count : count + 1, :slots] = diag


def split3(value):
    a = value.astype(jnp.bfloat16)
    rest = value - a.astype(jnp.float32)
    b = rest.astype(jnp.bfloat16)
    c = (rest - b.astype(jnp.float32)).astype(jnp.bfloat16)
    return a, b, c


def second_exchange(
    frames, message, infos, wanted, prior, windows, own, result,
    gathered, same, grad, grads, send, recv, gsend, grecv,
):
    n = lax.axis_size("bricks")
    me = lax.axis_index("bricks")
    groups = lax.axis_size("frames")
    slots = own.shape[0]
    meet(("bricks", "frames"))
    share_start("bricks", gathered, message, send, recv)
    gathered[me] = message[...]
    count = frames // (LANES // slots)
    for s in range(n):
        row = infos[s][count : count + 1, :]
        same[:, s * LANES : (s + 1) * LANES] = jnp.where(wanted[...] == row, 1.0, 0.0).astype(
            jnp.bfloat16
        )
    share_wait("bricks", gathered, message, send, recv)
    parts = [part.astype(jnp.float32) for part in split3(side_by_side(gathered))]
    parts = jnp.concatenate(parts, axis=0).astype(jnp.bfloat16)
    found = lax.dot_general(
        parts, same[...], (((1,), (1,)), ((), ())), preferred_element_type=jnp.float32
    )
    high = message.shape[0]
    found = found[:high] + found[high : 2 * high] + found[2 * high :]
    summed, diag = unpacked(found, frames, LANES // slots)
    new = jnp.maximum(0.0, prior[...] + summed / (diag + 1.0))
    result[:, 2 * LANES :] = jnp.zeros((slots, LANES), jnp.float32)
    result[:frames, 2 * LANES : 2 * LANES + new.shape[1] - slots] = new[:, slots:]
    turn = lax.broadcasted_iota(jnp.int32, (slots, slots), 0) == lax.broadcasted_iota(
        jnp.int32, (slots, slots), 1
    )
    picked = lax.dot_general(
        jnp.where(turn, 1.0, 0.0).astype(jnp.bfloat16),
        new[:, :slots].astype(jnp.bfloat16),
        (((1,), (1,)), ((), ())),
        preferred_element_type=jnp.float32,
    ).astype(jnp.bfloat16)
    gram = lax.dot_general(
        picked, picked, (((1,), (1,)), ((), ())), preferred_element_type=jnp.float32
    )
    g1, g2, g3 = split3(gram)
    none = jnp.zeros((slots, frames), jnp.float32)
    left = jnp.concatenate(
        [
            jnp.concatenate([picked.astype(jnp.float32), -g1.astype(jnp.float32)], axis=1),
            jnp.concatenate([none, -g2.astype(jnp.float32)], axis=1),
            jnp.concatenate([none, -g3.astype(jnp.float32)], axis=1),
        ],
        axis=0,
    ).astype(jnp.bfloat16)
    sub = lax.broadcasted_iota(jnp.int32, (slots, 2 * LANES), 0)
    total = jnp.zeros((slots, 2 * LANES), jnp.float32)
    for k in range(slots):
        one = jnp.dot(left, windows[k], preferred_element_type=jnp.float32)
        one = one[:slots] + one[slots : 2 * slots] + one[2 * slots :]
        total = jnp.where(sub == k, one, total)
    eye = lax.broadcasted_iota(jnp.int32, (slots, slots), 0) == lax.broadcasted_iota(
        jnp.int32, (slots, slots), 1
    )
    gdiag = jnp.sum(jnp.where(eye, gram, 0.0), axis=1, keepdims=True)
    grad[:, : 2 * LANES] = total
    grad[:, 2 * LANES :] = jnp.broadcast_to(gdiag, (slots, LANES))
    share_start("frames", grads, grad, gsend, grecv)
    grads[lax.axis_index("frames")] = grad[...]
    share_wait("frames", grads, grad, gsend, grecv)
    whole = grads[0]
    for g in range(1, groups):
        whole = whole + grads[g]
    current = own[...]
    step = whole[:, : 2 * LANES] / (whole[:, 2 * LANES : 2 * LANES + 1] + 1.0)
    result[:, : 2 * LANES] = jnp.where(current > 0, jnp.maximum(current + step, 0.0), 0.0)


def spread_kernel(tiles, at, result, out, new_out):
    slots, width = out.shape
    base = pl.program_id(0) * (width // LANES)
    first = at[...] - base
    second = jnp.where(at[...] + 1 == tiles, 0, at[...] + 1) - base
    head = result[:, :LANES]
    tail = result[:, LANES : 2 * LANES]
    for t in range(width // LANES):
        out[:, t * LANES : (t + 1) * LANES] = jnp.where(
            first == t, head, jnp.where(second == t, tail, 0.0)
        ).astype(jnp.bfloat16)
    frames, owned = new_out.shape
    new_out[...] = result[:frames, 2 * LANES : 2 * LANES + owned]


def shards(recording, traces, footprints, block_owner, block_slot):
    frames, planes, rows, width = recording.shape
    slots, voxels = footprints.shape
    owned = traces.shape[1]
    n = lax.axis_size("bricks")
    groups = lax.axis_size("frames")
    me = lax.axis_index("bricks")
    tiles = voxels // LANES
    f32 = jnp.float32
    sds = jax.ShapeDtypeStruct
    dma = pltpu.SemaphoreType.DMA
    component = block_owner[:, 0] * owned + block_slot
    rec = jnp.transpose(recording, (1, 2, 0, 3))
    packs = LANES // slots
    count = frames // packs
    high_rows = -(-(count + 1) // 8) * 8
    info = traces.astype(f32).reshape(packs, count, owned).transpose(1, 0, 2).reshape(count, LANES)
    extra = component[None, :] * packs + jnp.arange(packs, dtype=jnp.int32)[:, None]
    extra = jnp.pad(extra.astype(f32).reshape(1, LANES), ((0, high_rows - count - 1), (0, 0)))
    info = jnp.concatenate([info, extra], axis=0)
    order = jnp.arange(packs, dtype=jnp.int32)[:, None]
    columns = (component[None, :] * packs + order).reshape(packs * slots, 1)
    mine = me * owned + jnp.arange(owned, dtype=jnp.int32)
    both = jnp.concatenate([component, mine])
    wanted = (both[None, :] * packs + order).reshape(packs * (slots + owned), 1).astype(f32)

    y_tiles, infos, at = pl.pallas_call(
        first_exchange,
        out_shape=(
            sds((tiles, frames, LANES), jnp.bfloat16),
            sds((n,) + info.shape, f32),
            sds((slots, LANES), jnp.int32),
        ),
        in_specs=[VMEM] * 3,
        out_specs=(VMEM,) * 3,
        scratch_shapes=[
            pltpu.VMEM((SWEEPS, rows, frames, width), jnp.bfloat16),
            pltpu.VMEM((SWEEPS, rows, frames, width), jnp.bfloat16),
            pltpu.VMEM((planes + 4, rows, frames, width), f32),
            pltpu.VMEM((planes + 2, rows, frames, width), f32),
            dma((2, CUTS)),
            dma((2, CUTS)),
            dma((n,)),
            dma((n,)),
        ],
        compiler_params=pltpu.CompilerParams(
            collective_id=0, has_side_effects=True, vmem_limit_bytes=32 << 20
        ),
        name="first_exchange",
    )(rec, info, footprints)

    message, windows, own, slot_traces = pl.pallas_call(
        functools.partial(local_kernel, tiles),
        out_shape=(
            sds((high_rows, LANES), f32),
            sds((slots, frames + slots, 2 * LANES), jnp.bfloat16),
            sds((slots, 2 * LANES), f32),
            sds((frames, slots), f32),
        ),
        in_specs=[SMEM] + [VMEM] * 4,
        out_specs=(VMEM,) * 4,
        compiler_params=pltpu.CompilerParams(vmem_limit_bytes=32 << 20),
        name="project",
    )(at, y_tiles, footprints, infos, columns)

    prior = jnp.concatenate([slot_traces, traces.astype(f32)], axis=1)

    result = pl.pallas_call(
        functools.partial(second_exchange, frames),
        out_shape=sds((slots, 3 * LANES), f32),
        in_specs=[VMEM] * 6,
        out_specs=VMEM,
        scratch_shapes=[
            pltpu.VMEM((n, high_rows, LANES), f32),
            pltpu.VMEM((packs * (slots + owned), n * LANES), jnp.bfloat16),
            pltpu.VMEM((slots, 3 * LANES), f32),
            pltpu.VMEM((groups, slots, 3 * LANES), f32),
            dma((n,)),
            dma((n,)),
            dma((groups,)),
            dma((groups,)),
        ],
        compiler_params=pltpu.CompilerParams(
            collective_id=1, has_side_effects=True, vmem_limit_bytes=16 << 20
        ),
        name="second_exchange",
    )(message, infos, wanted, prior, windows, own)

    steps = 4 if tiles % 4 == 0 else 1
    footprints_new, traces_new = pl.pallas_call(
        functools.partial(spread_kernel, tiles),
        out_shape=(sds((slots, voxels), jnp.bfloat16), sds((frames, owned), f32)),
        grid=(steps,),
        in_specs=[
            pl.BlockSpec((slots, LANES), lambda i: (0, 0)),
            pl.BlockSpec((slots, 3 * LANES), lambda i: (0, 0)),
        ],
        out_specs=(
            pl.BlockSpec((slots, voxels // steps), lambda i: (0, i)),
            pl.BlockSpec((frames, owned), lambda i: (0, 0)),
        ),
        name="spread",
    )(at, result)
    return (traces_new, footprints_new)


def solution(mesh):
    return jax.shard_map(
        shards,
        mesh=mesh,
        in_specs=(
            P("frames", "bricks", None, None),
            P("frames", "bricks"),
            P("bricks", None),
            P("bricks", None),
            P("bricks"),
        ),
        out_specs=(P("frames", "bricks"), P("bricks", None)),
        check_vma=False,
    )
```
